512 devices in a mesh: latent: 128 (over x, z, core), tok: 4 (over y).
Axes of the slice: x: 4, y: 4, z: 16, core: 2. Of those that a mesh axis runs over, the one named last changes fastest.
Arguments:
- tokens: bfloat16 [16384, 8192], P('latent', 'tok'), may hold values from -6 to 6
- blocks: int32 [16384, 2], P('latent'), may hold values from 0 to 127, all different within a row; in each aligned block of 128 rows (0 to 127, 128 to 255, ...) at most 3 rows name the same one
- slots: int32 [16384, 64], P('latent'), may hold values from 0 to 255, all different within a row
- enc_weight: bfloat16 [16384, 8192], P('latent', 'tok'), may hold values from -0.0625 to 0.0625
- dec_weight: bfloat16 [16384, 8192], P('latent', 'tok'), may hold values from -0.75 to 0.75
- enc_bias: float32 [16384], P('latent'), may hold values from -3 to 3
Outputs:
- grad_enc: bfloat16 [16384, 8192], P('latent', 'tok')
- grad_dec: bfloat16 [16384, 8192], P('latent', 'tok')
The draws below stay inside these ranges and needn't reach their ends.
Inputs may be any that keep to these rules, and one draw needn't show every extreme that they name: Each row names 2 different blocks; the rows of one index of latent name one block at most 3 times. `slots`: each row names 64 different positions of the 2 blocks of its token; every position is named by some row.
All inputs are finite; a program needn't handle non-finite values.
Results may differ from the reference program's by a relative error of at most 0.0057.
Values may be sent and summed in bfloat16 or wider, within the bound.
A program may use at most 64 MiB of HBM per device.

```python
import math
import jax
import jax.numpy as jnp
import numpy as np
from jax import lax

D = 8192
K = 64
LAT = 128
NB = 2
T_DEV = 128
TOKENS = 16384
LATENTS = 16384
CAP = 3
N_LATENT = 128


def shard_levels(stream_key, extent, split, smallest, top_value):
    def one(axis_at, blocks):
        heights = jax.random.uniform(jax.random.fold_in(jax.random.fold_in(stream_key, 6), axis_at), (blocks,), jnp.float32, smallest / len(split), top_value / len(split))
        return jnp.repeat(jnp.exp(heights), extent[axis_at] // blocks).reshape((-1,) + (1,) * (len(extent) - axis_at - 1))

    factor_of = one(*split[0])
    for cut in split[1:]:
        factor_of = factor_of * one(*cut)
    return factor_of


def different_ones(own_key, rows, count, top, lift):
    ranking = jax.random.permutation(jax.random.fold_in(own_key, 1), count)
    favour = ranking
    for power in range(3):
        favour = favour * favour // count
    favour = favour * lift // count
    chance = jax.random.randint(jax.random.fold_in(own_key, 2), (rows, count), 0, 4096) + favour
    fixed_rows = jax.random.permutation(jax.random.fold_in(own_key, 3), rows)[jnp.arange(count) % rows]
    chance = jnp.where(jnp.arange(rows)[:, None] == fixed_rows[None, :], 1 << 14, chance)
    merit = chance * count + jnp.arange(count)
    return lax.top_k(merit.astype(jnp.int32), top)[1].astype(jnp.int32)


def routed_block(rng, own, number, rows, number_of, top, bound, lean):
    order = jax.random.permutation(rng, number_of)
    crowded, ordinary = load_shares(number_of, rows * top, bound, lean, True), load_shares(number_of, rows * top, bound, lean, False)
    places = jnp.arange(number_of)

    def named(lengths, rotation):
        used = int((lengths > 0).sum())
        fixed = max(1, used // 4)
        moved = fixed + (places - fixed + rotation * (used - fixed)) % max(1, number_of - fixed)
        return jnp.zeros((number_of,), jnp.int32).at[order[jnp.where(places < fixed, places, moved)]].set(jnp.asarray(lengths, jnp.int32))

    lengths = jnp.where(number % 4 == 0, named(crowded, number // 4), named(ordinary, number - number // 4 - 1))
    mixed = jax.random.permutation(jax.random.fold_in(own, 3), number_of)
    source_of, receiver = mixed[0:number_of // 2 * 2:2], mixed[1:number_of // 2 * 2:2]
    room = jnp.minimum(lengths[source_of] - 1, bound - lengths[receiver]) // 2
    room = jnp.where((source_of == order[0]) | (receiver == order[0]) | (lengths[receiver] == 0), 0, jnp.maximum(room, 0))
    moved = jax.random.randint(jax.random.fold_in(own, 4), (number_of // 2,), 0, 1 << 20) % (room + 1)
    lengths = lengths.at[source_of].add(-moved).at[receiver].add(moved)
    members = jnp.searchsorted(jnp.cumsum(lengths), jnp.arange(rows * top), side="right").astype(jnp.int32)
    grid = members.reshape(top, rows).T
    grid = grid[jax.random.permutation(jax.random.fold_in(own, 1), rows)]
    rotation = jax.random.randint(jax.random.fold_in(own, 2), (rows, 1), 0, top)
    return jnp.take_along_axis(grid, (jnp.arange(top)[None, :] + rotation) % top, axis=1)


def load_shares(count, total, reach, slope, full):
    loads = [(1 << 20) // math.isqrt(grade ** slope) + 1 for grade in range(1, count + 1)]
    largest = reach if full else min(reach, max(-(-total // count), total * loads[0] // sum(loads)))
    least = 1 if total - largest >= count - 1 else 0
    holding, rest = [largest] + [least] * (count - 1), total - largest - least * (count - 1)
    while rest > 0:
        movable = [i for i in range(1, count) if holding[i] < largest] or [i for i in range(1, count) if holding[i] < reach]
        whole, remaining = sum([loads[i] for i in movable]), rest
        for i in movable:
            more = min(reach - holding[i], max(1, remaining * loads[i] // whole), rest)
            holding[i] = holding[i] + more
            rest = rest - more
    return np.array(holding)


def normal_values(key, shape, width, bound, cuts=(), held_as=jnp.bfloat16):
    array = width * jax.random.normal(key, shape, jnp.float32)
    if cuts:
        array = array * shard_levels(key, shape, cuts, -0.22, 0.18)
    return jnp.clip(array, -bound, bound).astype(held_as)


def setup_inputs(seed: int = 0) -> dict:
    splits = jax.random.split(jax.random.key(seed), 7)
    tokens = normal_values(splits[0], (TOKENS, D), 1.0, 6.0, ((0, 128), (1, 4)))
    blocks_keys = jax.random.split(jax.random.fold_in(splits[1], 1), TOKENS // T_DEV)
    blocks_turns = jax.random.permutation(jax.random.fold_in(splits[1], 3), TOKENS // T_DEV)
    blocks = jax.vmap(lambda own, number: routed_block(jax.random.fold_in(splits[1], 2), own, number, T_DEV, N_LATENT, NB, CAP, 2))(blocks_keys, blocks_turns).reshape((TOKENS, NB))
    slots = different_ones(splits[2], TOKENS, NB * LAT, K, 0)
    enc_weight = normal_values(splits[3], (LATENTS, D), D ** -0.5, 0.0625, ((0, 128), (1, 4)))
    dec_weight = normal_values(splits[4], (LATENTS, D), K ** -0.5, 0.75, ((0, 128), (1, 4)))
    enc_bias = normal_values(splits[5], (LATENTS,), 0.5, 3.0, ((0, 128),), jnp.float32)
    return dict(tokens=tokens, blocks=blocks, slots=slots, enc_weight=enc_weight, dec_weight=dec_weight, enc_bias=enc_bias)


def reference(tokens, blocks, slots, enc_weight, dec_weight, enc_bias):
    pair_count = TOKENS * NB
    target = blocks.reshape(N_LATENT, T_DEV * NB)
    block_ids = jnp.arange(N_LATENT, dtype=jnp.int32)
    onehot = (target[:, :, None] == block_ids[None, None, :]).astype(jnp.int32)
    slot_rank = lax.optimization_barrier(jnp.sum(onehot * jnp.cumsum(onehot, axis=1), axis=2)) - 1
    source = jnp.broadcast_to(block_ids[:, None], target.shape)
    pair_ids = jnp.arange(pair_count, dtype=jnp.int32).reshape(N_LATENT, T_DEV * NB)
    table = jnp.full((N_LATENT, N_LATENT, CAP), pair_count, jnp.int32)
    table = table.at[target, source, slot_rank].set(pair_ids).reshape(N_LATENT, N_LATENT * CAP)
    row_index = jnp.arange(TOKENS, dtype=jnp.int32)[:, None]
    member = jnp.zeros((TOKENS, NB, LAT), jnp.float32).at[row_index, slots // LAT, slots % LAT].set(1.0)
    member = jnp.concatenate([member.reshape(pair_count, LAT), jnp.zeros((1, LAT), jnp.float32)], axis=0)
    grad_scale = math.sqrt(LAT / (T_DEV * K))

    def block_rows(block_index):
        pair_rows = table[block_index]
        token_index = jnp.minimum(pair_rows // NB, TOKENS - 1)
        mask_rows = member[pair_rows]
        start = (block_index * LAT).astype(jnp.int32)
        enc_rows = lax.dynamic_slice_in_dim(enc_weight, start, LAT, 0).astype(jnp.float32)
        dec_rows = lax.dynamic_slice_in_dim(dec_weight, start, LAT, 0).astype(jnp.float32)
        bias_rows = lax.dynamic_slice_in_dim(enc_bias, start, LAT, 0)
        return (pair_rows, token_index, mask_rows, enc_rows, dec_rows, bias_rows)

    def forward(recon, block_index):
        pair_rows, token_index, mask_rows, enc_rows, dec_rows, bias_rows = block_rows(block_index)
        inputs = tokens[token_index].astype(jnp.float32)
        pre_acts = jnp.dot(inputs, enc_rows.T, precision=lax.Precision.HIGHEST) + bias_rows[None, :]
        code_values = (mask_rows * pre_acts).astype(jnp.bfloat16)
        partial_value = jnp.dot(code_values.astype(jnp.float32), dec_rows, precision=lax.Precision.HIGHEST).astype(jnp.bfloat16)
        target_rows = jnp.where(pair_rows < pair_count, pair_rows // NB, TOKENS)
        recon = recon.at[target_rows].add(partial_value.astype(jnp.float32), mode='drop')
        return (recon, code_values)
    start_recon = jnp.zeros((TOKENS, D), jnp.float32)
    recon, all_codes = lax.scan(forward, start_recon, jnp.arange(N_LATENT, dtype=jnp.int32))
    error_rows = (recon - tokens.astype(jnp.float32)).astype(jnp.bfloat16)

    def backward(packed):
        block_index, code_values = packed
        pair_rows, token_index, mask_rows, enc_rows, dec_rows, bias_rows = block_rows(block_index)
        inputs = tokens[token_index].astype(jnp.float32)
        errors = error_rows[token_index].astype(jnp.float32)
        back_grad = (mask_rows * jnp.dot(errors, dec_rows.T, precision=lax.Precision.HIGHEST)).astype(jnp.bfloat16)
        dec_block = jnp.dot(code_values.astype(jnp.float32).T, errors, precision=lax.Precision.HIGHEST) * grad_scale
        enc_block = jnp.dot(back_grad.astype(jnp.float32).T, inputs, precision=lax.Precision.HIGHEST) * grad_scale
        return (enc_block.astype(jnp.bfloat16), dec_block.astype(jnp.bfloat16))
    grad_enc, grad_dec = lax.map(backward, (jnp.arange(N_LATENT, dtype=jnp.int32), all_codes))
    return (grad_enc.reshape(LATENTS, D), grad_dec.reshape(LATENTS, D))
```

```python
import functools
import math

import jax
import jax.numpy as jnp
from jax import lax
from jax.experimental import pallas as pl
from jax.experimental.pallas import tpu as pltpu
from jax.sharding import PartitionSpec as P

MESH = pl.DeviceIdType.MESH
F32 = jnp.float32
BF16 = jnp.bfloat16

NX, NZ, NC = 4, 16, 2
N = NX * NZ * NC
HALF = N // NC
CAP = 3
NY = 4
SUB = 16
LANE = 128
CHUNK = CAP * NZ


def latent_index(x, z, c):
    return (x * NZ + z) * NC + c


def inner_index(x, z, c):
    return (c * NX + x) * NZ + z


def z_step(k):
    return jnp.where(lax.rem(k, 2) == 1, (k + 1) // 2, NZ - k // 2)


def kernel(
    tokens, blocks, slots, enc, dec, bias,
    genc, gdec,
    sx, rx, sp, rp, se, re, sm, rm,
    nat, xnat, enat, st, smat, mem,
    part_f, part_b, sum_f, sum_b, codes, back, mask,
    sx_sem, sp_sem, se_sem, sm_sem, rx_sem, rp_sem, re_sem, rm_sem,
    sf_sem, rf_sem, sg_sem, rg_sem,
):
    width = tokens.shape[1]
    rows = tokens.shape[0]
    me = lax.axis_index("latent")
    y = lax.axis_index("tok")
    c = lax.rem(me, NC)
    z = lax.rem(me // NC, NZ)
    x = me // (NC * NZ)
    mine = inner_index(x, z, c)

    def partner(k):
        dz, rest = k // (NX * NC), lax.rem(k, NX * NC)
        px = lax.rem(x + rest // NC, NX)
        pz = lax.rem(z + z_step(dz), NZ)
        pc = lax.rem(c + lax.rem(rest, NC), NC)
        return px, pz, pc

    barrier = pltpu.get_barrier_semaphore()

    def greet(k, _):
        pl.semaphore_signal(
            barrier, inc=1, device_id={"latent": latent_index(*partner(k))}, device_id_type=MESH
        )
        return 0

    lax.fori_loop(1, N, greet, 0)
    for k in range(1, NY):
        pl.semaphore_signal(
            barrier, inc=1, device_id={"tok": lax.rem(y + k, NY)}, device_id_type=MESH
        )

    row = lax.broadcasted_iota(jnp.int32, (256, 256), 0)
    col = lax.broadcasted_iota(jnp.int32, (256, 256), 1)
    swap = jnp.where(
        (row // SUB == lax.rem(col, SUB)) & (lax.rem(row, SUB) == col // SUB), 1.0, 0.0
    ).astype(BF16)

    def to_tiles(src, row0, dst, place, rank):
        block = src[pl.ds(row0, SUB), :]
        stacked = jnp.concatenate(
            [block[:, i * LANE : (i + 1) * LANE] for i in range(width // LANE)], axis=0
        )
        out = jnp.dot(swap, stacked, preferred_element_type=F32).astype(BF16)
        dst[pl.ds(place, SUB), rank] = out.reshape(SUB, SUB, LANE)

    def to_rows(src, place, rank, dst, row0):
        block = src[pl.ds(place, SUB), rank].reshape(SUB * SUB, LANE)
        out = jnp.dot(swap, block, preferred_element_type=F32).astype(BF16)
        dst[pl.ds(row0, SUB), :] = jnp.concatenate(
            [out[i * SUB : (i + 1) * SUB, :] for i in range(width // LANE)], axis=1
        )

    lanes = lax.broadcasted_iota(jnp.int32, (rows, N), 1)
    subs = lax.broadcasted_iota(jnp.int32, (rows, N), 0)
    named = blocks[...]
    place = lax.rem(named, NC) * HALF + named // NC
    hot = [jnp.where(place[:, b : b + 1] == lanes, 1.0, 0.0) for b in range(2)]
    lower = jnp.where(lanes < subs, 1.0, 0.0).astype(BF16)
    ahead0 = jnp.dot(lower, hot[0].astype(BF16), preferred_element_type=F32)
    ahead1 = jnp.dot(lower, hot[1].astype(BF16), preferred_element_type=F32) + jnp.sum(
        hot[0], axis=0, keepdims=True
    )
    for r in range(CAP):
        s0 = hot[0] * jnp.where(ahead0 == r, 1.0, 0.0)
        s1 = hot[1] * jnp.where(ahead1 == r, 1.0, 0.0)
        st[:, r * N : (r + 1) * N] = (s0 + s1).astype(BF16)
        smat[0, r * N : (r + 1) * N, :] = s0.T.astype(BF16)
        smat[1, r * N : (r + 1) * N, :] = s1.T.astype(BF16)

    step = 512

    def spread(src):
        def one(i, _):
            cols = pl.ds(pl.multiple_of(i * step, step), step)
            both = smat[0] + smat[1]
            nat[:, cols] = jnp.dot(both, src[:, cols], preferred_element_type=F32).astype(BF16)
            return 0

        lax.fori_loop(0, width // step, one, 0)

    def pack(dst):
        def one(g, _):
            r, d = g // (N // SUB), lax.rem(g, N // SUB)
            to_tiles(nat, pl.multiple_of(g * SUB, SUB), dst, d * SUB, r)
            return 0

        lax.fori_loop(0, CAP * N // SUB, one, 0)

    def send_rows(src, dst, send_sem, recv_sem):
        pltpu.make_async_copy(src.at[mine], dst.at[mine], recv_sem.at[c]).start()

        def one(k, _):
            px, pz, pc = partner(k)
            pltpu.make_async_remote_copy(
                src_ref=src.at[inner_index(px, pz, pc)],
                dst_ref=dst.at[mine],
                send_sem=send_sem,
                recv_sem=recv_sem.at[c],
                device_id={"latent": latent_index(px, pz, pc)},
                device_id_type=MESH,
            ).start()
            return 0

        lax.fori_loop(1, N, one, 0)

    def take(ref, sem):
        pltpu.make_async_copy(ref, ref, sem).wait()

    spread(tokens)
    pack(sx)
    pl.semaphore_wait(barrier, N - 1 + NY - 1)

    @pl.when(c == 0)
    def _():
        send_rows(sx, rx, sx_sem, rx_sem)

    ids = slots[...]
    member = [jnp.zeros((rows, LANE), F32) for _ in range(2)]
    for k in range(slots.shape[1]):
        one_id = ids[:, k : k + 1]
        member = [jnp.where(one_id == lanes + b * LANE, 1.0, member[b]) for b in range(2)]
    for b in range(2):
        mem[b] = member[b].astype(BF16)
    slot_mask = (
        jnp.dot(smat[0], mem[0], preferred_element_type=F32)
        + jnp.dot(smat[1], mem[1], preferred_element_type=F32)
    ).astype(BF16)
    ri = lax.broadcasted_iota(jnp.int32, (SUB * SUB, CHUNK), 0)
    ci = lax.broadcasted_iota(jnp.int32, (SUB * SUB, CHUNK), 1)
    pick = jnp.where(
        (lax.rem(ri, SUB) == ci // SUB) & (ri // SUB == lax.rem(ci, SUB)), 1.0, 0.0
    ).astype(BF16)
    for g in range(N // SUB):
        three = jnp.concatenate(
            [slot_mask[r * N + g * SUB : r * N + (g + 1) * SUB, :] for r in range(CAP)], axis=0
        )
        out = jnp.dot(pick, three, preferred_element_type=F32).astype(BF16)
        sm[g * SUB : (g + 1) * SUB] = out.reshape(SUB, SUB, LANE)

    def send_mask():
        spot = c * NZ + z
        pltpu.make_async_copy(sm.at[mine], rm.at[spot], rm_sem.at[c]).start()

        def one(k, _):
            px, pz, pc = partner(k)
            pltpu.make_async_remote_copy(
                src_ref=sm.at[inner_index(px, pz, pc)],
                dst_ref=rm.at[spot],
                send_sem=sm_sem,
                recv_sem=rm_sem.at[c],
                device_id={"latent": latent_index(px, pz, pc)},
                device_id_type=MESH,
            ).start()
            return 0

        lax.fori_loop(1, N, one, 0)

    @pl.when((x == y) & (c == 0))
    def _():
        send_mask()

    def unpack(src, dst, h):
        def one(i, _):
            g = h * (HALF // SUB * CAP) + i
            to_rows(src, (g // CAP) * SUB, lax.rem(g, CAP), dst, pl.multiple_of(g * SUB, SUB))
            return 0

        lax.fori_loop(0, HALF // SUB * CAP, one, 0)

    def contract(left, right, h):
        lhs = left[pl.ds(h * NX * CHUNK, NX * CHUNK), :]
        out = lax.dot_general(lhs, right[...], (((1,), (1,)), ((), ())), preferred_element_type=F32)
        return out.reshape(NX, CHUNK, LANE)

    def scatter(part, total, h, q):
        for k in range(1, NY):
            p = lax.rem(y + k, NY)
            pltpu.make_async_remote_copy(
                src_ref=part.at[h, p],
                dst_ref=total.at[h, k],
                send_sem=sf_sem.at[q, h],
                recv_sem=rf_sem.at[q, h],
                device_id={"tok": p},
                device_id_type=MESH,
            ).start()

    def summed(part, total, h, q):
        take(total.at[h, pl.ds(1, NY - 1)], rf_sem.at[q, h])
        out = part[h, y]
        for k in range(1, NY):
            out = out + total[h, k]
        return out

    def gather(values, h, q):
        for k in range(1, NY):
            pltpu.make_async_remote_copy(
                src_ref=values.at[h, y],
                dst_ref=values.at[h, y],
                send_sem=sg_sem.at[q, h],
                recv_sem=rg_sem.at[q, h],
                device_id={"tok": lax.rem(y + k, NY)},
                device_id_type=MESH,
            ).start()

    def gathered(values, h, q):
        take(values.at[h, pl.ds(0, NY - 1)], rg_sem.at[q, h])

    def forward(h):
        unpack(rx, xnat, h)
        part_f[h] = contract(xnat, enc, h)
        scatter(part_f, sum_f, h, 0)
        take(rm.at[pl.ds(h * NZ, NZ)], rm_sem.at[h])
        got = rm[h * NZ : (h + 1) * NZ].reshape(NZ * SUB, LANE)
        mask[h] = lax.dot_general(pick, got, (((0,), (0,)), ((), ())), preferred_element_type=F32)
        total = summed(part_f, sum_f, h, 0)
        codes[h, y] = (mask[h] * (total + bias[...])).astype(BF16)
        gather(codes, h, 0)
        gathered(codes, h, 0)
        mine_codes = codes[h].reshape(NX * CHUNK, LANE)

        def product(i, _):
            cols = pl.ds(pl.multiple_of(i * step, step), step)
            nat[pl.ds(h * NX * CHUNK, NX * CHUNK), cols] = jnp.dot(
                mine_codes, dec[:, cols], preferred_element_type=F32
            ).astype(BF16)
            return 0

        lax.fori_loop(0, width // step, product, 0)

        def one(i, _):
            g = h * (HALF // SUB * CAP) + i
            to_tiles(nat, pl.multiple_of(g * SUB, SUB), sp, (g // CAP) * SUB, lax.rem(g, CAP))
            return 0

        lax.fori_loop(0, HALF // SUB * CAP, one, 0)

        def send(k, _):
            px, pz = lax.rem(x + lax.rem(k, NX), NX), lax.rem(z + z_step(k // NX), NZ)
            pltpu.make_async_remote_copy(
                src_ref=sp.at[inner_index(px, pz, h)],
                dst_ref=rp.at[mine],
                send_sem=sp_sem.at[h],
                recv_sem=rp_sem,
                device_id={"latent": latent_index(px, pz, h)},
                device_id_type=MESH,
            ).start()
            return 0

        @pl.when(c == h)
        def _():
            pltpu.make_async_copy(sp.at[mine], rp.at[mine], rp_sem).start()

        @pl.when(c != h)
        def _():
            send(0, 0)

        lax.fori_loop(1, HALF, send, 0)

    take(rx.at[pl.ds(0, HALF)], rx_sem.at[0])

    @pl.when(c == 1)
    def _():
        send_rows(sx, rx, sx_sem, rx_sem)

    @pl.when((x == y) & (c == 1))
    def _():
        send_mask()

    forward(0)
    take(rx.at[pl.ds(HALF, HALF)], rx_sem.at[1])
    forward(1)

    take(rp, rp_sem)

    def returned(g, _):
        r, d = g // (N // SUB), lax.rem(g, N // SUB)
        to_rows(rp, d * SUB, r, nat, pl.multiple_of(g * SUB, SUB))
        return 0

    lax.fori_loop(0, CAP * N // SUB, returned, 0)

    def error(i, _):
        cols = pl.ds(pl.multiple_of(i * step, step), step)
        recon = jnp.dot(st[...], nat[:, cols], preferred_element_type=F32)
        err = (recon - tokens[:, cols].astype(F32)).astype(BF16)
        nat[:, cols] = jnp.dot(
            smat[0] + smat[1], err, preferred_element_type=F32
        ).astype(BF16)
        return 0

    lax.fori_loop(0, width // step, error, 0)
    pack(se)
    send_rows(se, re, se_sem, re_sem)

    def backward(h):
        take(re.at[pl.ds(h * HALF, HALF)], re_sem.at[h])
        unpack(re, enat, h)
        part_b[h] = contract(enat, dec, h)
        scatter(part_b, sum_b, h, 1)
        total = summed(part_b, sum_b, h, 1)
        back[h, y] = (mask[h] * total).astype(BF16)
        gather(back, h, 1)

    backward(0)
    backward(1)
    scale = math.sqrt(LANE / (rows * slots.shape[1]))

    def gradient(values, other, out):
        left = values[...].reshape(CAP * N, LANE).astype(F32).T.astype(BF16)

        def one(i, _):
            cols = pl.ds(pl.multiple_of(i * step, step), step)
            out[:, cols] = (
                jnp.dot(left, other[:, cols], preferred_element_type=F32) * scale
            ).astype(BF16)
            return 0

        lax.fori_loop(0, width // step, one, 0)

    gradient(codes, enat, gdec)
    gathered(back, 0, 1)
    gathered(back, 1, 1)
    gradient(back, xnat, genc)

    take(sx.at[pl.ds(0, N - 1)], sx_sem)
    take(se.at[pl.ds(0, N - 1)], se_sem)

    @pl.when(x == y)
    def _():
        take(sm.at[pl.ds(0, N - 1)], sm_sem)

    for h in range(NC):

        @pl.when(c == h)
        def _(h=h):
            take(sp.at[pl.ds(0, HALF - 1)], sp_sem.at[h])

        @pl.when(c != h)
        def _(h=h):
            take(sp.at[pl.ds(0, HALF)], sp_sem.at[h])

        take(part_f.at[h, pl.ds(0, NY - 1)], sf_sem.at[0, h])
        take(part_b.at[h, pl.ds(0, NY - 1)], sf_sem.at[1, h])
        take(codes.at[h, pl.ds(0, NY - 1)], sg_sem.at[0, h])
        take(back.at[h, pl.ds(0, NY - 1)], sg_sem.at[1, h])


def local(tokens, blocks, slots, enc, dec, bias):
    rows, width = tokens.shape
    tiles = pltpu.VMEM((N, CAP, SUB, LANE), BF16)
    dense = pltpu.VMEM((CAP * N, width), BF16)
    shares = pltpu.VMEM((NC, NY, CHUNK, LANE), F32)
    shares16 = pltpu.VMEM((NC, NY, CHUNK, LANE), BF16)
    dma = pltpu.SemaphoreType.DMA
    return pl.pallas_call(
        kernel,
        out_shape=[jax.ShapeDtypeStruct((rows, width), BF16)] * 2,
        in_specs=[pl.BlockSpec(memory_space=pltpu.VMEM)] * 6,
        out_specs=[pl.BlockSpec(memory_space=pltpu.VMEM)] * 2,
        scratch_shapes=[tiles] * 6
        + [
            pltpu.VMEM((N, SUB, LANE), BF16),
            pltpu.VMEM((NC * NZ, SUB, LANE), BF16),
            dense,
            dense,
            dense,
            pltpu.VMEM((rows, CAP * N), BF16),
            pltpu.VMEM((2, CAP * N, rows), BF16),
            pltpu.VMEM((2, rows, LANE), BF16),
            shares,
            shares,
            shares,
            shares,
            shares16,
            shares16,
            pltpu.VMEM((NC, CHUNK, LANE), F32),
            dma,
            dma((NC,)),
            dma,
            dma,
            dma((NC,)),
            dma,
            dma((NC,)),
            dma((NC,)),
            dma((2, NC)),
            dma((2, NC)),
            dma((2, NC)),
            dma((2, NC)),
        ],
        compiler_params=pltpu.CompilerParams(
            collective_id=0, has_side_effects=True, vmem_limit_bytes=40 << 20
        ),
    )(tokens, blocks, slots, enc, dec, bias.reshape(1, -1))


def solution(mesh):
    placed = (
        P("latent", "tok"),
        P("latent", None),
        P("latent", None),
        P("latent", "tok"),
        P("latent", "tok"),
        P("latent"),
    )
    return jax.shard_map(
        local,
        mesh=mesh,
        in_specs=placed,
        out_specs=(P("latent", "tok"), P("latent", "tok")),
        check_vma=False,
    )
```

```python
import functools
import math

import jax
import jax.numpy as jnp
from jax import lax
from jax.experimental import pallas as pl
from jax.experimental.pallas import tpu as pltpu
from jax.sharding import PartitionSpec as P

MESH = pl.DeviceIdType.MESH
F32 = jnp.float32
BF16 = jnp.bfloat16

NX, NZ, NC = 4, 16, 2
N = NX * NZ * NC
HALF = N // NC
CAP = 3
NY = 4
SUB = 16
LANE = 128
CHUNK = CAP * NZ
SPLIT = N // 2
FIRST = 32


def latent_index(x, z, c):
    return (x * NZ + z) * NC + c


def inner_index(x, z, c):
    return c * HALF + lax.rem(z, NY) * SUB + z // NY * NX + x


def z_step(k):
    return jnp.where(lax.rem(k, 2) == 1, (k + 1) // 2, NZ - k // 2)


def kernel(
    tokens_hbm, blocks, slots, enc_hbm, dec_hbm, bias,
    genc, gdec,
    tokens, enc, dec,
    sx, rx, sp, rp, se, re, s1, r1, s2, r2,
    nat, xnat, enat, smat, early,
    part_f, part_b, sum_f, sum_b, codes, back, mask,
    sx_sem, sp_sem, se_sem, s1_sem, s2_sem, rx_sem, rp_sem, re_sem, r1_sem, r2_sem,
    sf_sem, rf_sem, sg_sem, rg_sem, in_sem,
):
    width = tokens.shape[1]
    rows = tokens.shape[0]
    me = lax.axis_index("latent")
    y = lax.axis_index("tok")
    c = lax.rem(me, NC)
    z = lax.rem(me // NC, NZ)
    x = me // (NC * NZ)
    mine = inner_index(x, z, c)

    def partner(k):
        dz, rest = k // (NX * NC), lax.rem(k, NX * NC)
        px = lax.rem(x + rest // NC, NX)
        pz = lax.rem(z + z_step(dz), NZ)
        pc = lax.rem(c + lax.rem(rest, NC), NC)
        return px, pz, pc

    loads = [
        pltpu.make_async_copy(src, dst, in_sem.at[i])
        for i, (src, dst) in enumerate(((tokens_hbm, tokens), (enc_hbm, enc), (dec_hbm, dec)))
    ]
    loads[0].start()

    barrier = pltpu.get_barrier_semaphore()

    def greet(k, _):
        pl.semaphore_signal(
            barrier, inc=1, device_id={"latent": latent_index(*partner(k))}, device_id_type=MESH
        )
        return 0

    lax.fori_loop(1, N, greet, 0)
    for k in range(1, NY):
        pl.semaphore_signal(
            barrier, inc=1, device_id={"tok": lax.rem(y + k, NY)}, device_id_type=MESH
        )

    parts = width // LANE

    def to_tiles(src, row0, dst, place, rank):
        dst[place : place + SUB, rank] = pltpu.einshape(
            "a(bc)->abc", src[row0 : row0 + SUB, :], b=parts, c=LANE
        )

    def to_rows(src, place, rank, dst, row0):
        dst[row0 : row0 + SUB, :] = pltpu.einshape("abc->a(bc)", src[place : place + SUB, rank])

    lanes = lax.broadcasted_iota(jnp.int32, (N, rows), 1)
    subs = lax.broadcasted_iota(jnp.int32, (N, rows), 0)
    named = blocks[...]
    column = named // NC
    place = inner_index(column // NZ, lax.rem(column, NZ), lax.rem(named, NC))
    hot = [jnp.where(place[b : b + 1, :] == subs, 1.0, 0.0) for b in range(2)]
    upper = jnp.where(subs < lanes, 1.0, 0.0).astype(BF16)
    ahead0 = jnp.dot(hot[0].astype(BF16), upper, preferred_element_type=F32)
    ahead1 = jnp.dot(hot[1].astype(BF16), upper, preferred_element_type=F32) + jnp.sum(
        hot[0], axis=1, keepdims=True
    )
    rank = [
        jnp.sum(hot[b] * ahead, axis=0, keepdims=True) for b, ahead in enumerate((ahead0, ahead1))
    ]
    for r in range(CAP):
        smat[r * N : (r + 1) * N, :] = sum(
            hot[b] * jnp.where(rank[b] == r, 1.0, 0.0) for b in range(2)
        ).astype(BF16)

    step = 512

    def spread(src):
        def one(i, _):
            cols = pl.ds(pl.multiple_of(i * step, step), step)
            nat[:, cols] = jnp.dot(smat[...], src[:, cols], preferred_element_type=F32).astype(BF16)
            return 0

        lax.fori_loop(0, width // step, one, 0)

    def pack(dst):
        for g in range(CAP * N // SUB):
            to_tiles(nat, g * SUB, dst, g % (N // SUB) * SUB, g // (N // SUB))

    def send_rows(src, dst, send_sem, recv_sem, first=0, last=N - 1):
        def one(i, _):
            k = N - 1 - i
            px, pz, pc = partner(k)
            pltpu.make_async_remote_copy(
                src_ref=src.at[inner_index(px, pz, pc)],
                dst_ref=dst.at[mine],
                send_sem=send_sem,
                recv_sem=recv_sem.at[c, k // SPLIT],
                device_id={"latent": latent_index(px, pz, pc)},
                device_id_type=MESH,
            ).start()
            return 0

        lax.fori_loop(first, last, one, 0)
        if last == N - 1:
            pltpu.make_async_copy(src.at[mine], dst.at[mine], recv_sem.at[c, 0]).start()

    def take(ref, sem):
        pltpu.make_async_copy(ref, ref, sem).wait()

    with jax.named_scope("spread_tokens"):
        loads[0].wait()
        loads[1].start()
        loads[2].start()
        spread(tokens)
        pack(sx)
    with jax.named_scope("entry_wait"):
        pl.semaphore_wait(barrier, N - 1 + NY - 1)

    @pl.when(c == 0)
    def _():
        send_rows(sx, rx, sx_sem, rx_sem, 0, FIRST)

    masked = lax.rem(z, NY) == y

    @pl.when(masked)
    def _():
        ids = slots[...]
        member = [jnp.zeros((LANE, rows), F32) for _ in range(2)]
        for k in range(slots.shape[0]):
            one_id = ids[k : k + 1, :]
            member = [jnp.where(one_id == subs + b * LANE, 1.0, member[b]) for b in range(2)]
        member = [m.astype(BF16) for m in member]
        sub16 = lax.broadcasted_iota(jnp.int32, (SUB, rows), 0)
        for px in range(NX):
            for pc in range(NC):
                goes = [place[b : b + 1, :] == inner_index(px, sub16, pc) for b in range(2)]
                for r in range(CAP):
                    s1[px, (pc * CAP + r) * SUB : (pc * CAP + r + 1) * SUB, :] = sum(
                        lax.dot_general(
                            jnp.where(goes[b] & (rank[b] == r), 1.0, 0.0).astype(BF16),
                            member[b],
                            (((1,), (1,)), ((), ())),
                            preferred_element_type=F32,
                        )
                        for b in range(2)
                    ).astype(BF16)
        for k in range(NX):
            px = lax.rem(x + k, NX)
            copy = pltpu.make_async_remote_copy(
                src_ref=s1.at[px],
                dst_ref=r1.at[c * NX + x],
                send_sem=s1_sem,
                recv_sem=r1_sem,
                device_id={"latent": latent_index(px, z, 1)},
                device_id_type=MESH,
            )
            if k:
                copy.start()
            else:
                pl.when(c == 0)(copy.start)

        @pl.when(c == 1)
        def _():
            pltpu.make_async_copy(s1.at[x], r1.at[NX + x], r1_sem).start()

    @pl.when(c == 0)
    def _():
        send_rows(sx, rx, sx_sem, rx_sem, FIRST)

    @pl.when(masked & (c == 1))
    def _():
        take(r1, r1_sem)
        ro = lax.broadcasted_iota(jnp.int32, (NZ * 2 * SUB, NC * NX * CHUNK), 0)
        co = lax.broadcasted_iota(jnp.int32, (NZ * 2 * SUB, NC * NX * CHUNK), 1)
        from_x, from_r, from_c, to_z = ro & 3, (ro >> 2) & 3, (ro >> 4) & 1, ro >> 5
        origin = (from_c * NX + from_x) * CHUNK + from_r * NZ + to_z
        order = jnp.where((from_r < CAP) & (co == origin), 1.0, 0.0).astype(BF16)
        for pc in range(NC):
            got = r1[:, pc * CHUNK : (pc + 1) * CHUNK, :].reshape(NC * NX * CHUNK, LANE)
            out = jnp.dot(order, got, preferred_element_type=F32).astype(BF16)
            s2[pc] = out.reshape(NZ, 2 * SUB, LANE)

        def one(k, _):
            pz, pc = lax.rem(z + z_step(k // NC), NZ), lax.rem(c + lax.rem(k, NC), NC)
            pltpu.make_async_remote_copy(
                src_ref=s2.at[pc, pz],
                dst_ref=r2.at[z // NY],
                send_sem=s2_sem,
                recv_sem=r2_sem,
                device_id={"latent": latent_index(x, pz, pc)},
                device_id_type=MESH,
            ).start()
            return 0

        lax.fori_loop(1, NZ * NC, one, 0)
        pltpu.make_async_copy(s2.at[1, z], r2.at[z // NY], r2_sem).start()

    def unpack(src, dst, h):
        for g in range(h * (HALF // SUB * CAP), (h + 1) * (HALF // SUB * CAP)):
            to_rows(src, g // CAP * SUB, g % CAP, dst, g * SUB)

    def contract(left, right, h):
        lhs = left[pl.ds(h * NX * CHUNK, NX * CHUNK), :]
        out = lax.dot_general(lhs, right[...], (((1,), (1,)), ((), ())), preferred_element_type=F32)
        return out.reshape(NX, CHUNK, LANE)

    def scatter(part, total, h, q):
        for k in range(1, NY):
            p = lax.rem(y + k, NY)
            pltpu.make_async_remote_copy(
                src_ref=part.at[h, p],
                dst_ref=total.at[h, k],
                send_sem=sf_sem.at[q, h],
                recv_sem=rf_sem.at[q, h],
                device_id={"tok": p},
                device_id_type=MESH,
            ).start()

    def summed(part, total, h, q):
        take(total.at[h, pl.ds(1, NY - 1)], rf_sem.at[q, h])
        out = part[h, y]
        for k in range(1, NY):
            out = out + total[h, k]
        return out

    def gather(values, h, q):
        for k in range(1, NY):
            pltpu.make_async_remote_copy(
                src_ref=values.at[h, y],
                dst_ref=values.at[h, y],
                send_sem=sg_sem.at[q, h],
                recv_sem=rg_sem.at[q, h],
                device_id={"tok": lax.rem(y + k, NY)},
                device_id_type=MESH,
            ).start()

    def gathered(values, h, q):
        take(values.at[h, pl.ds(0, NY - 1)], rg_sem.at[q, h])

    def forward(h):
        if h == 0:
            loads[1].wait()
        unpack(rx, xnat, h)
        part_f[h] = contract(xnat, enc, h)
        scatter(part_f, sum_f, h, 0)
        if h == 0:
            take(r2, r2_sem)
            ri = lax.broadcasted_iota(jnp.int32, (CHUNK, NY * SUB), 0)
            ci = lax.broadcasted_iota(jnp.int32, (CHUNK, NY * SUB), 1)
            pick = jnp.where(
                ci == ((ri >> 2) & 3) * SUB + (ri >> 4) * NX + (ri & 3), 1.0, 0.0
            ).astype(BF16)
            for i in range(NC):
                got = r2[:, i * SUB : (i + 1) * SUB, :].reshape(NY * SUB, LANE)
                mask[i] = jnp.dot(pick, got, preferred_element_type=F32)
        total = summed(part_f, sum_f, h, 0)
        codes[h, y] = (mask[h] * (total + bias[...])).astype(BF16)
        gather(codes, h, 0)
        gathered(codes, h, 0)
        if h == 0:
            loads[2].wait()
        mine_codes = codes[h].reshape(NX * CHUNK, LANE)

        def product(i, _):
            cols = pl.ds(pl.multiple_of(i * step, step), step)
            nat[pl.ds(h * NX * CHUNK, NX * CHUNK), cols] = jnp.dot(
                mine_codes, dec[:, cols], preferred_element_type=F32
            ).astype(BF16)
            return 0

        lax.fori_loop(0, width // step, product, 0)

        for g in range(h * (HALF // SUB * CAP), (h + 1) * (HALF // SUB * CAP)):
            to_tiles(nat, g * SUB, sp, g // CAP * SUB, g % CAP)

        def send(k, _):
            px, pz = lax.rem(x + lax.rem(k, NX), NX), lax.rem(z + z_step(k // NX), NZ)
            pltpu.make_async_remote_copy(
                src_ref=sp.at[inner_index(px, pz, h)],
                dst_ref=rp.at[mine],
                send_sem=sp_sem.at[h],
                recv_sem=rp_sem,
                device_id={"latent": latent_index(px, pz, h)},
                device_id_type=MESH,
            ).start()
            return 0

        @pl.when(c == h)
        def _():
            pltpu.make_async_copy(sp.at[mine], rp.at[mine], rp_sem).start()

        @pl.when(c != h)
        def _():
            send(0, 0)

        lax.fori_loop(0, HALF - 1, lambda i, _: send(HALF - 1 - i, _), 0)

    with jax.named_scope("rows_first_part"):
        take(rx.at[pl.ds(0, HALF // 2)], rx_sem.at[0, 1])

    @pl.when(c == 1)
    def _():
        send_rows(sx, rx, sx_sem, rx_sem)

    with jax.named_scope("rows_of_core_0"):
        take(rx.at[pl.ds(0, HALF // 2)], rx_sem.at[0, 0])
    with jax.named_scope("forward_core_0"):
        forward(0)
    with jax.named_scope("rows_of_core_1"):
        take(rx.at[pl.ds(HALF, HALF // 2)], rx_sem.at[1, 1])
        take(rx.at[pl.ds(HALF, HALF // 2)], rx_sem.at[1, 0])
    with jax.named_scope("forward_core_1"):
        forward(1)

    with jax.named_scope("partials"):
        take(rp, rp_sem)

    for g in range(CAP * N // SUB):
        to_rows(rp, g % (N // SUB) * SUB, g // (N // SUB), nat, g * SUB)

    collect = smat[...].astype(F32).T.astype(BF16)

    def error(i, _):
        cols = pl.ds(pl.multiple_of(i * step, step), step)
        recon = jnp.dot(collect, nat[:, cols], preferred_element_type=F32)
        err = (recon - tokens[:, cols].astype(F32)).astype(BF16)
        nat[:, cols] = jnp.dot(
            smat[...], err, preferred_element_type=F32
        ).astype(BF16)
        return 0

    with jax.named_scope("error_rows"):
        lax.fori_loop(0, width // step, error, 0)
        pack(se)
    with jax.named_scope("send_errors"):
        send_rows(se, re, se_sem, re_sem)

    scale = math.sqrt(LANE / (rows * slots.shape[0]))
    half_rows = NX * CHUNK

    def turned(values, h):
        return values[h].reshape(half_rows, LANE).astype(F32).T.astype(BF16)

    def arrived(h):
        with jax.named_scope("errors_of_core_%d" % h):
            take(re.at[pl.ds(h * HALF, HALF // 2)], re_sem.at[h, 1])
            take(re.at[pl.ds(h * HALF, HALF // 2)], re_sem.at[h, 0])
        unpack(re, enat, h)
        part_b[h] = contract(enat, dec, h)
        scatter(part_b, sum_b, h, 1)

    def finish(h):
        back[h, y] = (mask[h] * summed(part_b, sum_b, h, 1)).astype(BF16)
        gather(back, h, 1)

    def half_product(left, other, h, cols):
        return jnp.dot(
            left, other[h * half_rows : (h + 1) * half_rows, cols], preferred_element_type=F32
        )

    pieces = [slice(i * step, (i + 1) * step) for i in range(width // step)]
    code_rows = [turned(codes, h) for h in range(NC)]
    arrived(0)
    finish(0)
    arrived(1)
    for cols in pieces:
        gdec[:, cols] = (
            sum(half_product(code_rows[h], enat, h, cols) for h in range(NC)) * scale
        ).astype(BF16)
    finish(1)
    gathered(back, 0, 1)
    left = turned(back, 0)
    for cols in pieces:
        early[:, cols] = half_product(left, xnat, 0, cols)
    gathered(back, 1, 1)
    left = turned(back, 1)
    for cols in pieces:
        genc[:, cols] = ((early[:, cols] + half_product(left, xnat, 1, cols)) * scale).astype(BF16)

    take(sx.at[pl.ds(0, N - 1)], sx_sem)
    take(se.at[pl.ds(0, N - 1)], se_sem)

    @pl.when(masked)
    def _():
        take(s1.at[pl.ds(0, NX - 1)], s1_sem)

        @pl.when(c == 0)
        def _():
            take(s1.at[0], s1_sem)

        @pl.when(c == 1)
        def _():
            take(s2.at[0], s2_sem)
            take(s2.at[1, pl.ds(0, NZ - 1)], s2_sem)

    for h in range(NC):

        @pl.when(c == h)
        def _(h=h):
            take(sp.at[pl.ds(0, HALF - 1)], sp_sem.at[h])

        @pl.when(c != h)
        def _(h=h):
            take(sp.at[pl.ds(0, HALF)], sp_sem.at[h])

        take(part_f.at[h, pl.ds(0, NY - 1)], sf_sem.at[0, h])
        take(part_b.at[h, pl.ds(0, NY - 1)], sf_sem.at[1, h])
        take(codes.at[h, pl.ds(0, NY - 1)], sg_sem.at[0, h])
        take(back.at[h, pl.ds(0, NY - 1)], sg_sem.at[1, h])


def local(tokens, blocks, slots, enc, dec, bias):
    rows, width = tokens.shape
    tiles = pltpu.VMEM((N, CAP, SUB, LANE), BF16)
    dense = pltpu.VMEM((CAP * N, width), BF16)
    shares = pltpu.VMEM((NC, NY, CHUNK, LANE), F32)
    shares16 = pltpu.VMEM((NC, NY, CHUNK, LANE), BF16)
    dma = pltpu.SemaphoreType.DMA
    hbm, vmem = pltpu.HBM, pltpu.VMEM
    return pl.pallas_call(
        kernel,
        out_shape=[jax.ShapeDtypeStruct((rows, width), BF16)] * 2,
        in_specs=[pl.BlockSpec(memory_space=m) for m in (hbm, vmem, vmem, hbm, hbm, vmem)],
        out_specs=[pl.BlockSpec(memory_space=vmem)] * 2,
        scratch_shapes=[pltpu.VMEM((rows, width), BF16)] * 3
        + [tiles] * 6
        + [
            pltpu.VMEM((NX, NC * CHUNK, LANE), BF16),
            pltpu.VMEM((NC * NX, NC * CHUNK, LANE), BF16),
            pltpu.VMEM((NC, NZ, 2 * SUB, LANE), BF16),
            pltpu.VMEM((NY, 2 * SUB, LANE), BF16),
            dense,
            dense,
            dense,
            pltpu.VMEM((CAP * N, rows), BF16),
            pltpu.VMEM((rows, width), F32),
            shares,
            shares,
            shares,
            shares,
            shares16,
            shares16,
            pltpu.VMEM((NC, CHUNK, LANE), F32),
            dma,
            dma((NC,)),
            dma,
            dma,
            dma,
            dma((NC, 2)),
            dma,
            dma((NC, 2)),
            dma,
            dma,
            dma((2, NC)),
            dma((2, NC)),
            dma((2, NC)),
            dma((2, NC)),
            dma((3,)),
        ],
        compiler_params=pltpu.CompilerParams(
            collective_id=0, has_side_effects=True, vmem_limit_bytes=60 << 20
        ),
    )(tokens, blocks.T, slots.T, enc, dec, bias.reshape(1, -1))


def solution(mesh):
    placed = (
        P("latent", "tok"),
        P("latent", None),
        P("latent", None),
        P("latent", "tok"),
        P("latent", "tok"),
        P("latent"),
    )
    return jax.shard_map(
        local,
        mesh=mesh,
        in_specs=placed,
        out_specs=(P("latent", "tok"), P("latent", "tok")),
        check_vma=False,
    )
```

```python
import functools
import math

import jax
import jax.numpy as jnp
from jax import lax
from jax.experimental import pallas as pl
from jax.experimental.pallas import tpu as pltpu
from jax.sharding import PartitionSpec as P

MESH = pl.DeviceIdType.MESH
F32 = jnp.float32
BF16 = jnp.bfloat16

NX, NZ, NC = 4, 16, 2
N = NX * NZ * NC
HALF = N // NC
CAP = 3
NY = 4
SUB = 16
LANE = 128
CHUNK = CAP * NZ
SPLIT = 32
FIRST = 16
OTHERS = N - NZ


def latent_index(x, z, c):
    return (x * NZ + z) * NC + c


def inner_index(x, z, c):
    return c * HALF + lax.rem(z, NY) * SUB + z // NY * NX + x


def z_step(k):
    return jnp.where(lax.rem(k, 2) == 1, (k + 1) // 2, NZ - k // 2)


def kernel(
    tokens_hbm, blocks_hbm, slots_hbm, enc_hbm, dec_hbm, bias_hbm,
    genc, gdec,
    tokens, blocks, slots, enc, dec, bias,
    sx, rx, sp, rp, se, re, s1, r1, s2, r2,
    nat, xnat, enat, smat, early,
    part_f, part_b, sum_f, sent_b, sum_b, codes, back, mask, mask_all,
    sx_sem, sp_sem, se_sem, s1_sem, s2_sem, rx_sem, rp_sem, re_sem, r1_sem, r2_sem,
    sf_sem, rf_sem, sg_sem, rg_sem, in_sem, line_sem,
):
    width = tokens.shape[1]
    rows = tokens.shape[0]
    me = lax.axis_index("latent")
    y = lax.axis_index("tok")
    c = lax.rem(me, NC)
    z = lax.rem(me // NC, NZ)
    x = me // (NC * NZ)
    mine = inner_index(x, z, c)

    def partner(k):
        dz, rest = k // (NX * NC), lax.rem(k, NX * NC)
        px = lax.rem(x + rest // NC, NX)
        pz = lax.rem(z + z_step(dz), NZ)
        pc = lax.rem(c + lax.rem(rest, NC), NC)
        return px, pz, pc

    loads = [
        pltpu.make_async_copy(src, dst, in_sem.at[i])
        for i, (src, dst) in enumerate(
            (
                (tokens_hbm, tokens),
                (enc_hbm, enc),
                (dec_hbm, dec),
                (blocks_hbm, blocks),
                (slots_hbm, slots),
                (bias_hbm, bias),
            )
        )
    ]
    loads[3].start()
    loads[0].start()
    loads[4].start()
    loads[5].start()

    barrier = pltpu.get_barrier_semaphore()
    line_ids = [latent_index(x, lax.rem(z + k, NZ), c) for k in range(1, NZ)]
    plane_ids = [
        latent_index(lax.rem(x + k // NC, NX), z, lax.rem(c + k % NC, NC))
        for k in range(1, NX * NC)
    ]
    for peer in line_ids + plane_ids:
        pl.semaphore_signal(barrier, inc=1, device_id={"latent": peer}, device_id_type=MESH)
    for k in range(1, NY):
        pl.semaphore_signal(
            barrier, inc=1, device_id={"tok": lax.rem(y + k, NY)}, device_id_type=MESH
        )

    parts = width // LANE

    def to_tiles(src, row0, dst, place, rank):
        dst[place : place + SUB, rank] = pltpu.einshape(
            "a(bc)->abc", src[row0 : row0 + SUB, :], b=parts, c=LANE
        )

    def to_rows(src, place, rank, dst, row0):
        dst[row0 : row0 + SUB, :] = pltpu.einshape("abc->a(bc)", src[place : place + SUB, rank])

    lanes = lax.broadcasted_iota(jnp.int32, (N, rows), 1)
    subs = lax.broadcasted_iota(jnp.int32, (N, rows), 0)
    loads[3].wait()
    named = blocks[...]
    column = named // NC
    place = inner_index(column // NZ, lax.rem(column, NZ), lax.rem(named, NC))
    hot = [jnp.where(place[b : b + 1, :] == subs, 1.0, 0.0) for b in range(2)]
    upper = jnp.where(subs < lanes, 1.0, 0.0).astype(BF16)
    ahead0 = jnp.dot(hot[0].astype(BF16), upper, preferred_element_type=F32)
    ahead1 = jnp.dot(hot[1].astype(BF16), upper, preferred_element_type=F32) + jnp.sum(
        hot[0], axis=1, keepdims=True
    )
    rank = [
        jnp.sum(hot[b] * ahead, axis=0, keepdims=True) for b, ahead in enumerate((ahead0, ahead1))
    ]
    for r in range(CAP):
        smat[r * N : (r + 1) * N, :] = sum(
            hot[b] * jnp.where(rank[b] == r, 1.0, 0.0) for b in range(2)
        ).astype(BF16)

    step = 512

    def spread(src):
        def one(i, _):
            cols = pl.ds(pl.multiple_of(i * step, step), step)
            nat[:, cols] = jnp.dot(smat[...], src[:, cols], preferred_element_type=F32).astype(BF16)
            return 0

        lax.fori_loop(0, width // step, one, 0)

    def pack(dst):
        for g in range(CAP * N // SUB):
            to_tiles(nat, g * SUB, dst, g % (N // SUB) * SUB, g // (N // SUB))

    def send_rows(src, dst, send_sem, recv_sem, first, last):
        def one(k):
            px, pz, pc = partner(k)
            pltpu.make_async_remote_copy(
                src_ref=src.at[inner_index(px, pz, pc)],
                dst_ref=dst.at[mine],
                send_sem=send_sem,
                recv_sem=recv_sem.at[c, (k + N - SPLIT) // N],
                device_id={"latent": latent_index(px, pz, pc)},
                device_id_type=MESH,
            ).start()
            return 0

        group = NX * NC
        if first == 0:
            lax.fori_loop(0, NZ - 1, lambda i, _: one((NZ - 1 - i) * group), 0)
        others = lambda i, _: one((NZ - 1 - i // (group - 1)) * group + 1 + lax.rem(i, group - 1))
        lax.fori_loop(first or 0, last, others, 0)
        if last == OTHERS:
            pltpu.make_async_copy(src.at[mine], dst.at[mine], recv_sem.at[c, 0]).start()

    def take(ref, sem):
        pltpu.make_async_copy(ref, ref, sem).wait()

    with jax.named_scope("spread_tokens"):
        loads[0].wait()
        loads[4].wait()
        loads[5].wait()
        loads[1].start()
        loads[2].start()
        spread(tokens)
        pack(sx)
    with jax.named_scope("entry_wait"):
        pl.semaphore_wait(barrier, NZ - 1 + NX * NC - 1 + NY - 1)
    for peer in plane_ids:
        pl.semaphore_signal(line_sem, inc=1, device_id={"latent": peer}, device_id_type=MESH)

    @pl.when(c == 0)
    def _():
        send_rows(sx, rx, sx_sem, rx_sem, 0, 0)

    pl.semaphore_wait(line_sem, NX * NC - 1)

    @pl.when(c == 0)
    def _():
        send_rows(sx, rx, sx_sem, rx_sem, None, FIRST)

    masked = lax.rem(z, NY) == y

    @pl.when(masked)
    def _():
        ids = slots[...]
        member = [jnp.zeros((LANE, rows), F32) for _ in range(2)]
        for k in range(slots.shape[0]):
            one_id = ids[k : k + 1, :]
            member = [jnp.where(one_id == subs + b * LANE, 1.0, member[b]) for b in range(2)]
        member = [m.astype(BF16) for m in member]
        sub16 = lax.broadcasted_iota(jnp.int32, (SUB, rows), 0)
        for px in range(NX):
            for pc in range(NC):
                goes = [place[b : b + 1, :] == inner_index(px, sub16, pc) for b in range(2)]
                for r in range(CAP):
                    s1[px, (pc * CAP + r) * SUB : (pc * CAP + r + 1) * SUB, :] = sum(
                        lax.dot_general(
                            jnp.where(goes[b] & (rank[b] == r), 1.0, 0.0).astype(BF16),
                            member[b],
                            (((1,), (1,)), ((), ())),
                            preferred_element_type=F32,
                        )
                        for b in range(2)
                    ).astype(BF16)
        for k in range(NX):
            px = lax.rem(x + k, NX)
            copy = pltpu.make_async_remote_copy(
                src_ref=s1.at[px],
                dst_ref=r1.at[c * NX + x],
                send_sem=s1_sem,
                recv_sem=r1_sem,
                device_id={"latent": latent_index(px, z, 1)},
                device_id_type=MESH,
            )
            if k:
                copy.start()
            else:
                pl.when(c == 0)(copy.start)

        @pl.when(c == 1)
        def _():
            pltpu.make_async_copy(s1.at[x], r1.at[NX + x], r1_sem).start()

    @pl.when(c == 0)
    def _():
        send_rows(sx, rx, sx_sem, rx_sem, FIRST, OTHERS)

    @pl.when(masked & (c == 1))
    def _():
        take(r1, r1_sem)
        ro = lax.broadcasted_iota(jnp.int32, (NZ * 2 * SUB, NC * NX * CHUNK), 0)
        co = lax.broadcasted_iota(jnp.int32, (NZ * 2 * SUB, NC * NX * CHUNK), 1)
        from_x, from_r, from_c, to_z = ro & 3, (ro >> 2) & 3, (ro >> 4) & 1, ro >> 5
        origin = (from_c * NX + from_x) * CHUNK + from_r * NZ + to_z
        order = jnp.where((from_r < CAP) & (co == origin), 1.0, 0.0).astype(BF16)
        for pc in range(NC):
            got = r1[:, pc * CHUNK : (pc + 1) * CHUNK, :].reshape(NC * NX * CHUNK, LANE)
            out = jnp.dot(order, got, preferred_element_type=F32).astype(BF16)
            s2[pc] = out.reshape(NZ, 2 * SUB, LANE)

        def one(k, _):
            pz, pc = lax.rem(z + z_step(k // NC), NZ), lax.rem(c + lax.rem(k, NC), NC)
            pltpu.make_async_remote_copy(
                src_ref=s2.at[pc, pz],
                dst_ref=r2.at[z // NY],
                send_sem=s2_sem,
                recv_sem=r2_sem,
                device_id={"latent": latent_index(x, pz, pc)},
                device_id_type=MESH,
            ).start()
            return 0

        lax.fori_loop(1, NZ * NC, one, 0)
        pltpu.make_async_copy(s2.at[1, z], r2.at[z // NY], r2_sem).start()

    def unpack(src, dst, h):
        for g in range(h * (HALF // SUB * CAP), (h + 1) * (HALF // SUB * CAP)):
            to_rows(src, g // CAP * SUB, g % CAP, dst, g * SUB)

    def contract(left, right, h):
        lhs = left[pl.ds(h * NX * CHUNK, NX * CHUNK), :]
        out = lax.dot_general(lhs, right[...], (((1,), (1,)), ((), ())), preferred_element_type=F32)
        return out.reshape(NX, CHUNK, LANE)

    def scatter(part, total, h, q):
        for k in range(1, NY):
            p = lax.rem(y + k, NY)
            pltpu.make_async_remote_copy(
                src_ref=part.at[h, p],
                dst_ref=total.at[h, k],
                send_sem=sf_sem.at[q, h],
                recv_sem=rf_sem.at[q, h],
                device_id={"tok": p},
                device_id_type=MESH,
            ).start()

    def summed(part, total, h, q):
        take(total.at[h, pl.ds(1, NY - 1)], rf_sem.at[q, h])
        out = part[h, y]
        for k in range(1, NY):
            out = out + total[h, k]
        return out

    def gather(values, h, q):
        for k in range(1, NY):
            pltpu.make_async_remote_copy(
                src_ref=values.at[h, y],
                dst_ref=values.at[h, y],
                send_sem=sg_sem.at[q, h],
                recv_sem=rg_sem.at[q, h],
                device_id={"tok": lax.rem(y + k, NY)},
                device_id_type=MESH,
            ).start()

    def gathered(values, h, q):
        take(values.at[h, pl.ds(0, NY - 1)], rg_sem.at[q, h])

    def forward(h):
        if h == 0:
            loads[1].wait()
        unpack(rx, xnat, h)
        part_f[h] = contract(xnat, enc, h)
        scatter(part_f, sum_f, h, 0)
        if h == 0:
            take(r2, r2_sem)
            ri = lax.broadcasted_iota(jnp.int32, (CHUNK, NY * SUB), 0)
            ci = lax.broadcasted_iota(jnp.int32, (CHUNK, NY * SUB), 1)
            pick = jnp.where(
                ci == ((ri >> 2) & 3) * SUB + (ri >> 4) * NX + (ri & 3), 1.0, 0.0
            ).astype(BF16)
            for i in range(NC):
                got = r2[:, i * SUB : (i + 1) * SUB, :].reshape(NY * SUB, LANE)
                mask[i] = jnp.dot(pick, got, preferred_element_type=F32)
                mask_all[i, y] = mask[i].astype(BF16)
                gather(mask_all, i, 1)
        total = summed(part_f, sum_f, h, 0)
        codes[h, y] = (mask[h] * (total + bias[...])).astype(BF16)
        gather(codes, h, 0)
        gathered(codes, h, 0)
        if h == 0:
            loads[2].wait()
        mine_codes = codes[h].reshape(NX * CHUNK, LANE)

        def product(i, _):
            cols = pl.ds(pl.multiple_of(i * step, step), step)
            nat[pl.ds(h * NX * CHUNK, NX * CHUNK), cols] = jnp.dot(
                mine_codes, dec[:, cols], preferred_element_type=F32
            ).astype(BF16)
            return 0

        lax.fori_loop(0, width // step, product, 0)

        for g in range(h * (HALF // SUB * CAP), (h + 1) * (HALF // SUB * CAP)):
            to_tiles(nat, g * SUB, sp, g // CAP * SUB, g % CAP)

        def send(k, _):
            px, pz = lax.rem(x + lax.rem(k, NX), NX), lax.rem(z + z_step(k // NX), NZ)
            pltpu.make_async_remote_copy(
                src_ref=sp.at[inner_index(px, pz, h)],
                dst_ref=rp.at[mine],
                send_sem=sp_sem.at[h],
                recv_sem=rp_sem,
                device_id={"latent": latent_index(px, pz, h)},
                device_id_type=MESH,
            ).start()
            return 0

        @pl.when(c == h)
        def _():
            pltpu.make_async_copy(sp.at[mine], rp.at[mine], rp_sem).start()

        @pl.when(c != h)
        def _():
            send(0, 0)

        lax.fori_loop(0, HALF - 1, lambda i, _: send(HALF - 1 - i, _), 0)

    with jax.named_scope("rows_first_part"):
        take(rx.at[pl.ds(0, 48)], rx_sem.at[0, 1])

    @pl.when(c == 1)
    def _():
        send_rows(sx, rx, sx_sem, rx_sem, 0, OTHERS)

    with jax.named_scope("rows_of_core_0"):
        take(rx.at[pl.ds(0, 16)], rx_sem.at[0, 0])
    with jax.named_scope("forward_core_0"):
        forward(0)
    with jax.named_scope("rows_of_core_1"):
        take(rx.at[pl.ds(HALF, 48)], rx_sem.at[1, 1])
        take(rx.at[pl.ds(HALF, 16)], rx_sem.at[1, 0])
    with jax.named_scope("forward_core_1"):
        forward(1)

    with jax.named_scope("partials"):
        take(rp, rp_sem)

    for g in range(CAP * N // SUB):
        to_rows(rp, g % (N // SUB) * SUB, g // (N // SUB), nat, g * SUB)

    collect = smat[...].astype(F32).T.astype(BF16)

    def error(i, _):
        cols = pl.ds(pl.multiple_of(i * step, step), step)
        recon = jnp.dot(collect, nat[:, cols], preferred_element_type=F32)
        err = (recon - tokens[:, cols].astype(F32)).astype(BF16)
        nat[:, cols] = jnp.dot(
            smat[...], err, preferred_element_type=F32
        ).astype(BF16)
        return 0

    with jax.named_scope("error_rows"):
        lax.fori_loop(0, width // step, error, 0)
        pack(se)
    with jax.named_scope("send_errors"):
        send_rows(se, re, se_sem, re_sem, 0, OTHERS)

    scale = math.sqrt(LANE / (rows * slots.shape[0]))
    half_rows = NX * CHUNK

    def turned(values, h):
        return values[h].reshape(half_rows, LANE).astype(F32).T.astype(BF16)

    def arrived(h):
        with jax.named_scope("errors_of_core_%d" % h):
            take(re.at[pl.ds(h * HALF, 48)], re_sem.at[h, 1])
            take(re.at[pl.ds(h * HALF, 16)], re_sem.at[h, 0])
        unpack(re, enat, h)
        part_b[h] = contract(enat, dec, h)
        sent_b[h] = part_b[h].astype(BF16)
        for k in range(1, NY):
            pltpu.make_async_remote_copy(
                src_ref=sent_b.at[h],
                dst_ref=sum_b.at[h, k],
                send_sem=sf_sem.at[1, h],
                recv_sem=rf_sem.at[1, h],
                device_id={"tok": lax.rem(y + k, NY)},
                device_id_type=MESH,
            ).start()

    def finish(h):
        take(sum_b.at[h, pl.ds(1, NY - 1)], rf_sem.at[1, h])
        total = part_b[h]
        for k in range(1, NY):
            total = total + sum_b[h, k].astype(F32)
        back[h] = (mask_all[h].astype(F32) * total).astype(BF16)

    def half_product(left, other, h, cols):
        return jnp.dot(
            left, other[h * half_rows : (h + 1) * half_rows, cols], preferred_element_type=F32
        )

    pieces = [slice(i * step, (i + 1) * step) for i in range(width // step)]
    code_rows = [turned(codes, h) for h in range(NC)]
    arrived(0)
    arrived(1)
    for h in range(NC):
        gathered(mask_all, h, 1)
    finish(0)
    for cols in pieces:
        gdec[:, cols] = (
            sum(half_product(code_rows[h], enat, h, cols) for h in range(NC)) * scale
        ).astype(BF16)
    left = turned(back, 0)
    for cols in pieces:
        early[:, cols] = half_product(left, xnat, 0, cols)
    finish(1)
    left = turned(back, 1)
    for cols in pieces:
        genc[:, cols] = ((early[:, cols] + half_product(left, xnat, 1, cols)) * scale).astype(BF16)

    take(sx.at[pl.ds(0, N - 1)], sx_sem)
    take(se.at[pl.ds(0, N - 1)], se_sem)

    @pl.when(masked)
    def _():
        take(s1.at[pl.ds(0, NX - 1)], s1_sem)

        @pl.when(c == 0)
        def _():
            take(s1.at[0], s1_sem)

        @pl.when(c == 1)
        def _():
            take(s2.at[0], s2_sem)
            take(s2.at[1, pl.ds(0, NZ - 1)], s2_sem)

    for h in range(NC):

        @pl.when(c == h)
        def _(h=h):
            take(sp.at[pl.ds(0, HALF - 1)], sp_sem.at[h])

        @pl.when(c != h)
        def _(h=h):
            take(sp.at[pl.ds(0, HALF)], sp_sem.at[h])

        take(part_f.at[h, pl.ds(0, NY - 1)], sf_sem.at[0, h])
        take(sum_b.at[h, pl.ds(1, NY - 1)], sf_sem.at[1, h])
        take(codes.at[h, pl.ds(0, NY - 1)], sg_sem.at[0, h])
        take(mask_all.at[h, pl.ds(0, NY - 1)], sg_sem.at[1, h])


def local(tokens, blocks, slots, enc, dec, bias):
    rows, width = tokens.shape
    tiles = pltpu.VMEM((N, CAP, SUB, LANE), BF16)
    dense = pltpu.VMEM((CAP * N, width), BF16)
    shares = pltpu.VMEM((NC, NY, CHUNK, LANE), F32)
    shares16 = pltpu.VMEM((NC, NY, CHUNK, LANE), BF16)
    dma = pltpu.SemaphoreType.DMA
    hbm, vmem = pltpu.HBM, pltpu.VMEM
    args = (tokens, blocks.T, slots.T, enc, dec, bias.reshape(1, -1))
    return pl.pallas_call(
        kernel,
        out_shape=[jax.ShapeDtypeStruct((rows, width), BF16)] * 2,
        in_specs=[pl.BlockSpec(memory_space=hbm)] * 6,
        out_specs=[pl.BlockSpec(memory_space=vmem)] * 2,
        scratch_shapes=[pltpu.VMEM(a.shape, a.dtype) for a in args]
        + [tiles] * 6
        + [
            pltpu.VMEM((NX, NC * CHUNK, LANE), BF16),
            pltpu.VMEM((NC * NX, NC * CHUNK, LANE), BF16),
            pltpu.VMEM((NC, NZ, 2 * SUB, LANE), BF16),
            pltpu.VMEM((NY, 2 * SUB, LANE), BF16),
            dense,
            dense,
            dense,
            pltpu.VMEM((CAP * N, rows), BF16),
            pltpu.VMEM((rows, width), F32),
            shares,
            shares,
            shares,
            shares16,
            pltpu.VMEM((NC, NY, NY, CHUNK, LANE), BF16),
            shares16,
            shares16,
            pltpu.VMEM((NC, CHUNK, LANE), F32),
            shares16,
            dma,
            dma((NC,)),
            dma,
            dma,
            dma,
            dma((NC, 2)),
            dma,
            dma((NC, 2)),
            dma,
            dma,
            dma((2, NC)),
            dma((2, NC)),
            dma((2, NC)),
            dma((2, NC)),
            dma((6,)),
            pltpu.SemaphoreType.REGULAR,
        ],
        compiler_params=pltpu.CompilerParams(
            collective_id=0, has_side_effects=True, vmem_limit_bytes=36 << 20
        ),
    )(*[pltpu.with_memory_space_constraint(a, hbm) for a in args])


def solution(mesh):
    placed = (
        P("latent", "tok"),
        P("latent", None),
        P("latent", None),
        P("latent", "tok"),
        P("latent", "tok"),
        P("latent"),
    )
    return jax.shard_map(
        local,
        mesh=mesh,
        in_specs=placed,
        out_specs=(P("latent", "tok"), P("latent", "tok")),
        check_vma=False,
    )
```

```python
import functools
import math

import jax
import jax.numpy as jnp
from jax import lax
from jax.experimental import pallas as pl
from jax.experimental.pallas import tpu as pltpu
from jax.sharding import PartitionSpec as P

MESH = pl.DeviceIdType.MESH
F32 = jnp.float32
BF16 = jnp.bfloat16

NX, NZ, NC = 4, 16, 2
N = NX * NZ * NC
HALF = N // NC
CAP = 3
NY = 4
SUB = 16
LANE = 128
CHUNK = CAP * NZ
SPLIT = 48
FIRST = 16
OTHERS = N - NZ


def latent_index(x, z, c):
    return (x * NZ + z) * NC + c


def inner_index(x, z, c):
    return c * HALF + lax.rem(z, NY) * SUB + z // NY * NX + x


def z_step(k):
    return jnp.where(lax.rem(k, 2) == 1, (k + 1) // 2, NZ - k // 2)


def kernel(
    tokens_hbm, blocks_hbm, slots_hbm, enc_hbm, dec_hbm, bias_hbm,
    genc, gdec,
    tokens, blocks, slots, enc, dec, bias,
    sx, rx, sp, rp, se, re, s1, r1, s2, r2,
    nat, xnat, enat, smat, early,
    part_f, part_b, sum_f, sent_b, sum_b, codes, back, mask, mask_all,
    sx_sem, sp_sem, se_sem, s1_sem, s2_sem, rx_sem, rp_sem, re_sem, r1_sem, r2_sem,
    sf_sem, rf_sem, sg_sem, rg_sem, in_sem, line_sem,
):
    width = tokens.shape[1]
    rows = tokens.shape[0]
    me = lax.axis_index("latent")
    y = lax.axis_index("tok")
    c = lax.rem(me, NC)
    z = lax.rem(me // NC, NZ)
    x = me // (NC * NZ)
    mine = inner_index(x, z, c)

    def partner(k):
        dz, rest = k // (NX * NC), lax.rem(k, NX * NC)
        px = lax.rem(x + rest // NC, NX)
        pz = lax.rem(z + z_step(dz), NZ)
        pc = lax.rem(c + lax.rem(rest, NC), NC)
        return px, pz, pc

    loads = [
        pltpu.make_async_copy(src, dst, in_sem.at[i])
        for i, (src, dst) in enumerate(
            (
                (tokens_hbm, tokens),
                (enc_hbm, enc),
                (dec_hbm, dec),
                (blocks_hbm, blocks),
                (slots_hbm, slots),
                (bias_hbm, bias),
            )
        )
    ]
    loads[3].start()
    loads[0].start()
    loads[4].start()
    loads[5].start()

    barrier = pltpu.get_barrier_semaphore()
    line_ids = [latent_index(x, lax.rem(z + k, NZ), c) for k in range(1, NZ)]
    plane_ids = [
        latent_index(lax.rem(x + k // NC, NX), z, lax.rem(c + k % NC, NC))
        for k in range(1, NX * NC)
    ]
    for peer in line_ids + plane_ids:
        pl.semaphore_signal(barrier, inc=1, device_id={"latent": peer}, device_id_type=MESH)
    for k in range(1, NY):
        pl.semaphore_signal(
            barrier, inc=1, device_id={"tok": lax.rem(y + k, NY)}, device_id_type=MESH
        )

    parts = width // LANE

    def to_tiles(src, row0, dst, place, rank):
        dst[place : place + SUB, rank] = pltpu.einshape(
            "a(bc)->abc", src[row0 : row0 + SUB, :], b=parts, c=LANE
        )

    def to_rows(src, place, rank, dst, row0):
        dst[row0 : row0 + SUB, :] = pltpu.einshape("abc->a(bc)", src[place : place + SUB, rank])

    lanes = lax.broadcasted_iota(jnp.int32, (N, rows), 1)
    subs = lax.broadcasted_iota(jnp.int32, (N, rows), 0)
    loads[3].wait()
    named = blocks[...]
    column = named // NC
    place = inner_index(column // NZ, lax.rem(column, NZ), lax.rem(named, NC))
    hot = [jnp.where(place[b : b + 1, :] == subs, 1.0, 0.0) for b in range(2)]
    upper = jnp.where(subs < lanes, 1.0, 0.0).astype(BF16)
    ahead0 = jnp.dot(hot[0].astype(BF16), upper, preferred_element_type=F32)
    ahead1 = jnp.dot(hot[1].astype(BF16), upper, preferred_element_type=F32) + jnp.sum(
        hot[0], axis=1, keepdims=True
    )
    rank = [
        jnp.sum(hot[b] * ahead, axis=0, keepdims=True) for b, ahead in enumerate((ahead0, ahead1))
    ]
    for r in range(CAP):
        smat[r * N : (r + 1) * N, :] = sum(
            hot[b] * jnp.where(rank[b] == r, 1.0, 0.0) for b in range(2)
        ).astype(BF16)

    step = 512
    pieces = [slice(i * step, (i + 1) * step) for i in range(width // step)]

    def spread(src):
        for cols in pieces:
            nat[:, cols] = jnp.dot(smat[...], src[:, cols], preferred_element_type=F32).astype(BF16)

    def pack(dst):
        for g in range(CAP * N // SUB):
            to_tiles(nat, g * SUB, dst, g % (N // SUB) * SUB, g // (N // SUB))

    def send_rows(src, dst, send_sem, recv_sem, first, last):
        def one(k):
            px, pz, pc = partner(k)
            pltpu.make_async_remote_copy(
                src_ref=src.at[inner_index(px, pz, pc)],
                dst_ref=dst.at[mine],
                send_sem=send_sem,
                recv_sem=recv_sem.at[c, (k + N - SPLIT) // N],
                device_id={"latent": latent_index(px, pz, pc)},
                device_id_type=MESH,
            ).start()
            return 0

        group = NX * NC
        if first == 0:
            lax.fori_loop(0, NZ - 1, lambda i, _: one((NZ - 1 - i) * group), 0)
        others = lambda i, _: one((NZ - 1 - i // (group - 1)) * group + 1 + lax.rem(i, group - 1))
        lax.fori_loop(first or 0, last, others, 0)
        if last == OTHERS:
            pltpu.make_async_copy(src.at[mine], dst.at[mine], recv_sem.at[c, 0]).start()

    def take(ref, sem):
        pltpu.make_async_copy(ref, ref, sem).wait()

    with jax.named_scope("spread_tokens"):
        loads[0].wait()
        loads[4].wait()
        loads[5].wait()
        loads[1].start()
        loads[2].start()
        spread(tokens)
        pack(sx)
    with jax.named_scope("entry_wait"):
        pl.semaphore_wait(barrier, NZ - 1 + NX * NC - 1 + NY - 1)
    for peer in plane_ids:
        pl.semaphore_signal(line_sem, inc=1, device_id={"latent": peer}, device_id_type=MESH)

    @pl.when(c == 0)
    def _():
        send_rows(sx, rx, sx_sem, rx_sem, 0, 0)

    pl.semaphore_wait(line_sem, NX * NC - 1)

    @pl.when(c == 0)
    def _():
        send_rows(sx, rx, sx_sem, rx_sem, None, FIRST)

    masked = lax.rem(z, NY) == y

    @pl.when(masked)
    def _():
        ids = slots[...]
        member = [jnp.zeros((LANE, rows), F32) for _ in range(2)]
        for k in range(slots.shape[0]):
            one_id = ids[k : k + 1, :]
            member = [jnp.where(one_id == subs + b * LANE, 1.0, member[b]) for b in range(2)]
        member = [m.astype(BF16) for m in member]
        sub16 = lax.broadcasted_iota(jnp.int32, (SUB, rows), 0)
        for px in range(NX):
            for pc in range(NC):
                goes = [place[b : b + 1, :] == inner_index(px, sub16, pc) for b in range(2)]
                for r in range(CAP):
                    s1[px, (pc * CAP + r) * SUB : (pc * CAP + r + 1) * SUB, :] = sum(
                        lax.dot_general(
                            jnp.where(goes[b] & (rank[b] == r), 1.0, 0.0).astype(BF16),
                            member[b],
                            (((1,), (1,)), ((), ())),
                            preferred_element_type=F32,
                        )
                        for b in range(2)
                    ).astype(BF16)
        for k in range(NX):
            px = lax.rem(x + k, NX)
            copy = pltpu.make_async_remote_copy(
                src_ref=s1.at[px],
                dst_ref=r1.at[c * NX + x],
                send_sem=s1_sem,
                recv_sem=r1_sem,
                device_id={"latent": latent_index(px, z, 1)},
                device_id_type=MESH,
            )
            if k:
                copy.start()
            else:
                pl.when(c == 0)(copy.start)

        @pl.when(c == 1)
        def _():
            pltpu.make_async_copy(s1.at[x], r1.at[NX + x], r1_sem).start()

    @pl.when(c == 0)
    def _():
        send_rows(sx, rx, sx_sem, rx_sem, FIRST, OTHERS)

    @pl.when(masked & (c == 1))
    def _():
        take(r1, r1_sem)
        ro = lax.broadcasted_iota(jnp.int32, (NZ * 2 * SUB, NC * NX * CHUNK), 0)
        co = lax.broadcasted_iota(jnp.int32, (NZ * 2 * SUB, NC * NX * CHUNK), 1)
        from_x, from_r, from_c, to_z = ro & 3, (ro >> 2) & 3, (ro >> 4) & 1, ro >> 5
        origin = (from_c * NX + from_x) * CHUNK + from_r * NZ + to_z
        order = jnp.where((from_r < CAP) & (co == origin), 1.0, 0.0).astype(BF16)
        for pc in range(NC):
            got = r1[:, pc * CHUNK : (pc + 1) * CHUNK, :].reshape(NC * NX * CHUNK, LANE)
            out = jnp.dot(order, got, preferred_element_type=F32).astype(BF16)
            s2[pc] = out.reshape(NZ, 2 * SUB, LANE)

        def one(k, _):
            pz, pc = lax.rem(z + z_step(k // NC), NZ), lax.rem(c + lax.rem(k, NC), NC)
            pltpu.make_async_remote_copy(
                src_ref=s2.at[pc, pz],
                dst_ref=r2.at[z // NY],
                send_sem=s2_sem,
                recv_sem=r2_sem,
                device_id={"latent": latent_index(x, pz, pc)},
                device_id_type=MESH,
            ).start()
            return 0

        lax.fori_loop(1, NZ * NC, one, 0)
        pltpu.make_async_copy(s2.at[1, z], r2.at[z // NY], r2_sem).start()

    def unpack(src, dst, h):
        for g in range(h * (HALF // SUB * CAP), (h + 1) * (HALF // SUB * CAP)):
            to_rows(src, g // CAP * SUB, g % CAP, dst, g * SUB)

    def contract(left, right, h):
        lhs = left[pl.ds(h * NX * CHUNK, NX * CHUNK), :]
        out = lax.dot_general(lhs, right[...], (((1,), (1,)), ((), ())), preferred_element_type=F32)
        return out.reshape(NX, CHUNK, LANE)

    def scatter(part, total, h, q):
        for k in range(1, NY):
            p = lax.rem(y + k, NY)
            pltpu.make_async_remote_copy(
                src_ref=part.at[h, p],
                dst_ref=total.at[h, k],
                send_sem=sf_sem.at[q, h],
                recv_sem=rf_sem.at[q, h],
                device_id={"tok": p},
                device_id_type=MESH,
            ).start()

    def summed(part, total, h, q):
        take(total.at[h, pl.ds(1, NY - 1)], rf_sem.at[q, h])
        out = part[h, y]
        for k in range(1, NY):
            out = out + total[h, k]
        return out

    def gather(values, h, q):
        for k in range(1, NY):
            pltpu.make_async_remote_copy(
                src_ref=values.at[h, y],
                dst_ref=values.at[h, y],
                send_sem=sg_sem.at[q, h],
                recv_sem=rg_sem.at[q, h],
                device_id={"tok": lax.rem(y + k, NY)},
                device_id_type=MESH,
            ).start()

    def gathered(values, h, q):
        take(values.at[h, pl.ds(0, NY - 1)], rg_sem.at[q, h])

    def forward(h):
        if h == 0:
            loads[1].wait()
        unpack(rx, xnat, h)
        part_f[h] = contract(xnat, enc, h)
        scatter(part_f, sum_f, h, 0)
        if h == 0:
            take(r2, r2_sem)
            ri = lax.broadcasted_iota(jnp.int32, (CHUNK, NY * SUB), 0)
            ci = lax.broadcasted_iota(jnp.int32, (CHUNK, NY * SUB), 1)
            pick = jnp.where(
                ci == ((ri >> 2) & 3) * SUB + (ri >> 4) * NX + (ri & 3), 1.0, 0.0
            ).astype(BF16)
            for i in range(NC):
                got = r2[:, i * SUB : (i + 1) * SUB, :].reshape(NY * SUB, LANE)
                mask[i] = jnp.dot(pick, got, preferred_element_type=F32)
                mask_all[i, y] = mask[i].astype(BF16)
                gather(mask_all, i, 1)
        total = summed(part_f, sum_f, h, 0)
        codes[h, y] = (mask[h] * (total + bias[...])).astype(BF16)
        gather(codes, h, 0)
        gathered(codes, h, 0)
        if h == 0:
            loads[2].wait()
        mine_codes = codes[h].reshape(NX * CHUNK, LANE)

        for cols in pieces:
            nat[h * NX * CHUNK : (h + 1) * NX * CHUNK, cols] = jnp.dot(
                mine_codes, dec[:, cols], preferred_element_type=F32
            ).astype(BF16)

        for g in range(h * (HALF // SUB * CAP), (h + 1) * (HALF // SUB * CAP)):
            to_tiles(nat, g * SUB, sp, g // CAP * SUB, g % CAP)

        def send(k, _):
            px, pz = lax.rem(x + lax.rem(k, NX), NX), lax.rem(z + z_step(k // NX), NZ)
            pltpu.make_async_remote_copy(
                src_ref=sp.at[inner_index(px, pz, h)],
                dst_ref=rp.at[mine],
                send_sem=sp_sem.at[h],
                recv_sem=rp_sem,
                device_id={"latent": latent_index(px, pz, h)},
                device_id_type=MESH,
            ).start()
            return 0

        @pl.when(c == h)
        def _():
            pltpu.make_async_copy(sp.at[mine], rp.at[mine], rp_sem).start()

        @pl.when(c != h)
        def _():
            send(0, 0)

        lax.fori_loop(0, HALF - 1, lambda i, _: send(HALF - 1 - i, _), 0)

    with jax.named_scope("rows_first_part"):
        take(rx.at[pl.ds(0, 40)], rx_sem.at[0, 1])

    @pl.when(c == 1)
    def _():
        send_rows(sx, rx, sx_sem, rx_sem, 0, OTHERS)

    with jax.named_scope("rows_of_core_0"):
        take(rx.at[pl.ds(0, 24)], rx_sem.at[0, 0])
    with jax.named_scope("forward_core_0"):
        forward(0)
    with jax.named_scope("rows_of_core_1"):
        take(rx.at[pl.ds(HALF, 40)], rx_sem.at[1, 1])
        take(rx.at[pl.ds(HALF, 24)], rx_sem.at[1, 0])
    with jax.named_scope("forward_core_1"):
        forward(1)

    with jax.named_scope("partials"):
        take(rp, rp_sem)

    for g in range(CAP * N // SUB):
        to_rows(rp, g % (N // SUB) * SUB, g // (N // SUB), nat, g * SUB)

    collect = smat[...].astype(F32).T.astype(BF16)

    def error(cols):
        recon = jnp.dot(collect, nat[:, cols], preferred_element_type=F32)
        err = (recon - tokens[:, cols].astype(F32)).astype(BF16)
        nat[:, cols] = jnp.dot(
            smat[...], err, preferred_element_type=F32
        ).astype(BF16)

    with jax.named_scope("error_rows"):
        for cols in pieces:
            error(cols)
        pack(se)
    with jax.named_scope("send_errors"):
        send_rows(se, re, se_sem, re_sem, 0, OTHERS)

    half_rows = NX * CHUNK

    def turned(values, h):
        return values[h].reshape(half_rows, LANE).astype(F32).T.astype(BF16)

    def arrived(h):
        with jax.named_scope("errors_of_core_%d" % h):
            take(re.at[pl.ds(h * HALF, 40)], re_sem.at[h, 1])
            take(re.at[pl.ds(h * HALF, 24)], re_sem.at[h, 0])
        unpack(re, enat, h)
        part_b[h] = contract(enat, dec, h)
        sent_b[h] = part_b[h].astype(BF16)
        for k in range(1, NY):
            pltpu.make_async_remote_copy(
                src_ref=sent_b.at[h],
                dst_ref=sum_b.at[h, k],
                send_sem=sf_sem.at[1, h],
                recv_sem=rf_sem.at[1, h],
                device_id={"tok": lax.rem(y + k, NY)},
                device_id_type=MESH,
            ).start()

    def finish(h):
        take(sum_b.at[h, pl.ds(1, NY - 1)], rf_sem.at[1, h])
        total = part_b[h]
        for k in range(1, NY):
            total = total + sum_b[h, k].astype(F32)
        back[h] = (mask_all[h].astype(F32) * total).astype(BF16)

    def half_product(left, other, h, cols):
        return jnp.dot(
            left, other[h * half_rows : (h + 1) * half_rows, cols], preferred_element_type=F32
        )

    code_rows = [turned(codes, h) for h in range(NC)]
    arrived(0)
    arrived(1)
    for h in range(NC):
        gathered(mask_all, h, 1)
    finish(0)
    for cols in pieces:
        gdec[:, cols] = (
            sum(half_product(code_rows[h], enat, h, cols) for h in range(NC))
        ).astype(BF16)
    left = turned(back, 0)
    for cols in pieces:
        early[:, cols] = half_product(left, xnat, 0, cols)
    finish(1)
    left = turned(back, 1)
    for cols in pieces:
        genc[:, cols] = (early[:, cols] + half_product(left, xnat, 1, cols)).astype(BF16)

    take(sx.at[pl.ds(0, N - 1)], sx_sem)
    take(se.at[pl.ds(0, N - 1)], se_sem)

    @pl.when(masked)
    def _():
        take(s1.at[pl.ds(0, NX - 1)], s1_sem)

        @pl.when(c == 0)
        def _():
            take(s1.at[0], s1_sem)

        @pl.when(c == 1)
        def _():
            take(s2.at[0], s2_sem)
            take(s2.at[1, pl.ds(0, NZ - 1)], s2_sem)

    for h in range(NC):

        @pl.when(c == h)
        def _(h=h):
            take(sp.at[pl.ds(0, HALF - 1)], sp_sem.at[h])

        @pl.when(c != h)
        def _(h=h):
            take(sp.at[pl.ds(0, HALF)], sp_sem.at[h])

        take(part_f.at[h, pl.ds(0, NY - 1)], sf_sem.at[0, h])
        take(sum_b.at[h, pl.ds(1, NY - 1)], sf_sem.at[1, h])
        take(codes.at[h, pl.ds(0, NY - 1)], sg_sem.at[0, h])
        take(mask_all.at[h, pl.ds(0, NY - 1)], sg_sem.at[1, h])


def local(tokens, blocks, slots, enc, dec, bias):
    rows, width = tokens.shape
    tiles = pltpu.VMEM((N, CAP, SUB, LANE), BF16)
    dense = pltpu.VMEM((CAP * N, width), BF16)
    shares = pltpu.VMEM((NC, NY, CHUNK, LANE), F32)
    shares16 = pltpu.VMEM((NC, NY, CHUNK, LANE), BF16)
    dma = pltpu.SemaphoreType.DMA
    hbm, vmem = pltpu.HBM, pltpu.VMEM
    args = (tokens, blocks.T, slots.T, enc, dec, bias.reshape(1, -1))
    genc, gdec = pl.pallas_call(
        kernel,
        out_shape=[jax.ShapeDtypeStruct((rows, width), BF16)] * 2,
        in_specs=[pl.BlockSpec(memory_space=hbm)] * 6,
        out_specs=[pl.BlockSpec(memory_space=vmem)] * 2,
        scratch_shapes=[pltpu.VMEM(a.shape, a.dtype) for a in args]
        + [tiles] * 6
        + [
            pltpu.VMEM((NX, NC * CHUNK, LANE), BF16),
            pltpu.VMEM((NC * NX, NC * CHUNK, LANE), BF16),
            pltpu.VMEM((NC, NZ, 2 * SUB, LANE), BF16),
            pltpu.VMEM((NY, 2 * SUB, LANE), BF16),
            dense,
            dense,
            dense,
            pltpu.VMEM((CAP * N, rows), BF16),
            pltpu.VMEM((rows, width), F32),
            shares,
            shares,
            shares,
            shares16,
            pltpu.VMEM((NC, NY, NY, CHUNK, LANE), BF16),
            shares16,
            shares16,
            pltpu.VMEM((NC, CHUNK, LANE), F32),
            shares16,
            dma,
            dma((NC,)),
            dma,
            dma,
            dma,
            dma((NC, 2)),
            dma,
            dma((NC, 2)),
            dma,
            dma,
            dma((2, NC)),
            dma((2, NC)),
            dma((2, NC)),
            dma((2, NC)),
            dma((6,)),
            pltpu.SemaphoreType.REGULAR,
        ],
        compiler_params=pltpu.CompilerParams(
            collective_id=0, has_side_effects=True, vmem_limit_bytes=36 << 20
        ),
    )(*[pltpu.with_memory_space_constraint(a, hbm) for a in args])
    scale = jnp.asarray(math.sqrt(LANE / (rows * slots.shape[1])), BF16)
    return genc * scale, gdec * scale


def solution(mesh):
    placed = (
        P("latent", "tok"),
        P("latent", None),
        P("latent", None),
        P("latent", "tok"),
        P("latent", "tok"),
        P("latent"),
    )
    return jax.shard_map(
        local,
        mesh=mesh,
        in_specs=placed,
        out_specs=(P("latent", "tok"), P("latent", "tok")),
        check_vma=False,
    )
```

```python
import functools
import math

import jax
import jax.numpy as jnp
from jax import lax
from jax.experimental import pallas as pl
from jax.experimental.pallas import tpu as pltpu
from jax.sharding import PartitionSpec as P

MESH = pl.DeviceIdType.MESH
F32 = jnp.float32
BF16 = jnp.bfloat16

NX, NZ, NC = 4, 16, 2
N = NX * NZ * NC
HALF = N // NC
CAP = 3
NY = 4
SUB = 16
LANE = 128
CHUNK = CAP * NZ
SPLIT = 48
FIRST = 16
OTHERS = N - NZ


def latent_index(x, z, c):
    return (x * NZ + z) * NC + c


def inner_index(x, z, c):
    return c * HALF + lax.rem(z, NY) * SUB + z // NY * NX + x


def z_step(k):
    return jnp.where(lax.rem(k, 2) == 1, (k + 1) // 2, NZ - k // 2)


def kernel(
    tokens_hbm, blocks_hbm, slots_hbm, enc_hbm, dec_hbm, bias_hbm,
    genc, gdec,
    tokens, blocks, slots, enc, dec, bias,
    sx, rx, sp, rp, se, re, s1, r1, s2, r2,
    nat, xnat, enat, smat, early,
    part_f, part_b, sum_f, sent_b, sum_b, codes, back, mask, mask_all,
    sx_sem, sp_sem, se_sem, s1_sem, s2_sem, rx_sem, rp_sem, re_sem, r1_sem, r2_sem,
    sf_sem, rf_sem, sg_sem, rg_sem, in_sem, line_sem,
):
    width = tokens.shape[1]
    rows = tokens.shape[0]
    me = lax.axis_index("latent")
    y = lax.axis_index("tok")
    c = lax.rem(me, NC)
    z = lax.rem(me // NC, NZ)
    x = me // (NC * NZ)
    mine = inner_index(x, z, c)

    def partner(k):
        dz, rest = k // (NX * NC), lax.rem(k, NX * NC)
        px = lax.rem(x + rest // NC, NX)
        pz = lax.rem(z + z_step(dz), NZ)
        pc = lax.rem(c + lax.rem(rest, NC), NC)
        return px, pz, pc

    loads = [
        pltpu.make_async_copy(src, dst, in_sem.at[i])
        for i, (src, dst) in enumerate(
            (
                (tokens_hbm, tokens),
                (enc_hbm, enc),
                (dec_hbm, dec),
                (blocks_hbm, blocks),
                (slots_hbm, slots),
                (bias_hbm, bias),
            )
        )
    ]
    loads[3].start()
    loads[0].start()
    loads[4].start()
    loads[5].start()

    barrier = pltpu.get_barrier_semaphore()
    line_ids = [latent_index(x, lax.rem(z + k, NZ), c) for k in range(1, NZ)]
    plane_ids = [
        latent_index(lax.rem(x + k // NC, NX), z, lax.rem(c + k % NC, NC))
        for k in range(1, NX * NC)
    ]
    for peer in line_ids + plane_ids:
        pl.semaphore_signal(barrier, inc=1, device_id={"latent": peer}, device_id_type=MESH)
    for k in range(1, NY):
        pl.semaphore_signal(
            barrier, inc=1, device_id={"tok": lax.rem(y + k, NY)}, device_id_type=MESH
        )

    parts = width // LANE

    def to_tiles(src, row0, dst, place, rank):
        dst[place : place + SUB, rank] = pltpu.einshape(
            "a(bc)->abc", src[row0 : row0 + SUB, :], b=parts, c=LANE
        )

    def to_rows(src, place, rank, dst, row0):
        dst[row0 : row0 + SUB, :] = pltpu.einshape("abc->a(bc)", src[place : place + SUB, rank])

    lanes = lax.broadcasted_iota(jnp.int32, (N, rows), 1)
    subs = lax.broadcasted_iota(jnp.int32, (N, rows), 0)
    loads[3].wait()
    named = blocks[...]
    column = named // NC
    place = inner_index(column // NZ, lax.rem(column, NZ), lax.rem(named, NC))
    hot = [jnp.where(place[b : b + 1, :] == subs, 1.0, 0.0) for b in range(2)]
    upper = jnp.where(subs < lanes, 1.0, 0.0).astype(BF16)
    ahead0 = jnp.dot(hot[0].astype(BF16), upper, preferred_element_type=F32)
    ahead1 = jnp.dot(hot[1].astype(BF16), upper, preferred_element_type=F32) + jnp.sum(
        hot[0], axis=1, keepdims=True
    )
    rank = [
        jnp.sum(hot[b] * ahead, axis=0, keepdims=True) for b, ahead in enumerate((ahead0, ahead1))
    ]
    for r in range(CAP):
        smat[r * N : (r + 1) * N, :] = sum(
            hot[b] * jnp.where(rank[b] == r, 1.0, 0.0) for b in range(2)
        ).astype(BF16)

    step = 512
    pieces = [slice(i * step, (i + 1) * step) for i in range(width // step)]

    def spread(src):
        for cols in pieces:
            nat[:, cols] = jnp.dot(smat[...], src[:, cols], preferred_element_type=F32).astype(BF16)

    def pack(dst):
        for g in range(CAP * N // SUB):
            to_tiles(nat, g * SUB, dst, g % (N // SUB) * SUB, g // (N // SUB))

    def send_rows(src, dst, send_sem, recv_sem, first, last):
        def one(k):
            px, pz, pc = partner(k)
            pltpu.make_async_remote_copy(
                src_ref=src.at[inner_index(px, pz, pc)],
                dst_ref=dst.at[mine],
                send_sem=send_sem,
                recv_sem=recv_sem.at[c, (k + N - SPLIT) // N],
                device_id={"latent": latent_index(px, pz, pc)},
                device_id_type=MESH,
            ).start()
            return 0

        group = NX * NC
        if first == 0:
            lax.fori_loop(0, NZ - 1, lambda i, _: one((NZ - 1 - i) * group), 0)
        others = lambda i, _: one((NZ - 1 - i // (group - 1)) * group + 1 + lax.rem(i, group - 1))
        lax.fori_loop(first or 0, last, others, 0)
        if last == OTHERS:
            pltpu.make_async_copy(src.at[mine], dst.at[mine], recv_sem.at[c, 0]).start()

    def take(ref, sem):
        pltpu.make_async_copy(ref, ref, sem).wait()

    with jax.named_scope("spread_tokens"):
        loads[0].wait()
        loads[4].wait()
        loads[5].wait()
        loads[1].start()
        loads[2].start()
        spread(tokens)
        pack(sx)
    with jax.named_scope("entry_wait"):
        pl.semaphore_wait(barrier, NZ - 1 + NX * NC - 1 + NY - 1)
    for peer in plane_ids:
        pl.semaphore_signal(line_sem, inc=1, device_id={"latent": peer}, device_id_type=MESH)

    @pl.when(c == 0)
    def _():
        send_rows(sx, rx, sx_sem, rx_sem, 0, 0)

    @pl.when(c == 1)
    def _():
        send_rows(sx, rx, sx_sem, rx_sem, 0, 0)

    pl.semaphore_wait(line_sem, NX * NC - 1)

    @pl.when(c == 0)
    def _():
        send_rows(sx, rx, sx_sem, rx_sem, None, FIRST)

    masked = lax.rem(z, NY) == y

    @pl.when(masked)
    def _():
        ids = slots[...]
        member = [jnp.zeros((LANE, rows), F32) for _ in range(2)]
        for k in range(slots.shape[0]):
            one_id = ids[k : k + 1, :]
            member = [jnp.where(one_id == subs + b * LANE, 1.0, member[b]) for b in range(2)]
        member = [m.astype(BF16) for m in member]
        sub16 = lax.broadcasted_iota(jnp.int32, (SUB, rows), 0)
        for px in range(NX):
            for pc in range(NC):
                goes = [place[b : b + 1, :] == inner_index(px, sub16, pc) for b in range(2)]
                for r in range(CAP):
                    s1[px, (pc * CAP + r) * SUB : (pc * CAP + r + 1) * SUB, :] = sum(
                        lax.dot_general(
                            jnp.where(goes[b] & (rank[b] == r), 1.0, 0.0).astype(BF16),
                            member[b],
                            (((1,), (1,)), ((), ())),
                            preferred_element_type=F32,
                        )
                        for b in range(2)
                    ).astype(BF16)
        for k in range(NX):
            px = lax.rem(x + k, NX)
            copy = pltpu.make_async_remote_copy(
                src_ref=s1.at[px],
                dst_ref=r1.at[c * NX + x],
                send_sem=s1_sem,
                recv_sem=r1_sem,
                device_id={"latent": latent_index(px, z, 1)},
                device_id_type=MESH,
            )
            if k:
                copy.start()
            else:
                pl.when(c == 0)(copy.start)

        @pl.when(c == 1)
        def _():
            pltpu.make_async_copy(s1.at[x], r1.at[NX + x], r1_sem).start()

    @pl.when(c == 0)
    def _():
        send_rows(sx, rx, sx_sem, rx_sem, FIRST, OTHERS)

    @pl.when(masked & (c == 1))
    def _():
        take(r1, r1_sem)
        ro = lax.broadcasted_iota(jnp.int32, (NZ * 2 * SUB, NC * NX * CHUNK), 0)
        co = lax.broadcasted_iota(jnp.int32, (NZ * 2 * SUB, NC * NX * CHUNK), 1)
        from_x, from_r, from_c, to_z = ro & 3, (ro >> 2) & 3, (ro >> 4) & 1, ro >> 5
        origin = (from_c * NX + from_x) * CHUNK + from_r * NZ + to_z
        order = jnp.where((from_r < CAP) & (co == origin), 1.0, 0.0).astype(BF16)
        for pc in range(NC):
            got = r1[:, pc * CHUNK : (pc + 1) * CHUNK, :].reshape(NC * NX * CHUNK, LANE)
            out = jnp.dot(order, got, preferred_element_type=F32).astype(BF16)
            s2[pc] = out.reshape(NZ, 2 * SUB, LANE)

        def one(k, _):
            pz, pc = lax.rem(z + z_step(k // NC), NZ), lax.rem(c + lax.rem(k, NC), NC)
            pltpu.make_async_remote_copy(
                src_ref=s2.at[pc, pz],
                dst_ref=r2.at[z // NY],
                send_sem=s2_sem,
                recv_sem=r2_sem,
                device_id={"latent": latent_index(x, pz, pc)},
                device_id_type=MESH,
            ).start()
            return 0

        lax.fori_loop(1, NZ * NC, one, 0)
        pltpu.make_async_copy(s2.at[1, z], r2.at[z // NY], r2_sem).start()

    def unpack(src, dst, h):
        for g in range(h * (HALF // SUB * CAP), (h + 1) * (HALF // SUB * CAP)):
            to_rows(src, g // CAP * SUB, g % CAP, dst, g * SUB)

    def contract(left, right, h):
        lhs = left[pl.ds(h * NX * CHUNK, NX * CHUNK), :]
        out = lax.dot_general(lhs, right[...], (((1,), (1,)), ((), ())), preferred_element_type=F32)
        return out.reshape(NX, CHUNK, LANE)

    def scatter(part, total, h, q):
        for k in range(1, NY):
            p = lax.rem(y + k, NY)
            pltpu.make_async_remote_copy(
                src_ref=part.at[h, p],
                dst_ref=total.at[h, k],
                send_sem=sf_sem.at[q, h],
                recv_sem=rf_sem.at[q, h],
                device_id={"tok": p},
                device_id_type=MESH,
            ).start()

    def summed(part, total, h, q):
        take(total.at[h, pl.ds(1, NY - 1)], rf_sem.at[q, h])
        out = part[h, y]
        for k in range(1, NY):
            out = out + total[h, k]
        return out

    def gather(values, h, q):
        for k in range(1, NY):
            pltpu.make_async_remote_copy(
                src_ref=values.at[h, y],
                dst_ref=values.at[h, y],
                send_sem=sg_sem.at[q, h],
                recv_sem=rg_sem.at[q, h],
                device_id={"tok": lax.rem(y + k, NY)},
                device_id_type=MESH,
            ).start()

    def gathered(values, h, q):
        take(values.at[h, pl.ds(0, NY - 1)], rg_sem.at[q, h])

    def forward(h):
        if h == 0:
            loads[1].wait()
        unpack(rx, xnat, h)
        part_f[h] = contract(xnat, enc, h)
        scatter(part_f, sum_f, h, 0)
        if h == 0:
            take(r2, r2_sem)
            ri = lax.broadcasted_iota(jnp.int32, (CHUNK, NY * SUB), 0)
            ci = lax.broadcasted_iota(jnp.int32, (CHUNK, NY * SUB), 1)
            pick = jnp.where(
                ci == ((ri >> 2) & 3) * SUB + (ri >> 4) * NX + (ri & 3), 1.0, 0.0
            ).astype(BF16)
            for i in range(NC):
                got = r2[:, i * SUB : (i + 1) * SUB, :].reshape(NY * SUB, LANE)
                mask[i] = jnp.dot(pick, got, preferred_element_type=F32)
                mask_all[i, y] = mask[i].astype(BF16)
                gather(mask_all, i, 1)
        total = summed(part_f, sum_f, h, 0)
        codes[h, y] = (mask[h] * (total + bias[...])).astype(BF16)
        gather(codes, h, 0)
        gathered(codes, h, 0)
        if h == 0:
            loads[2].wait()
        mine_codes = codes[h].reshape(NX * CHUNK, LANE)

        for cols in pieces:
            nat[h * NX * CHUNK : (h + 1) * NX * CHUNK, cols] = jnp.dot(
                mine_codes, dec[:, cols], preferred_element_type=F32
            ).astype(BF16)

        for g in range(h * (HALF // SUB * CAP), (h + 1) * (HALF // SUB * CAP)):
            to_tiles(nat, g * SUB, sp, g // CAP * SUB, g % CAP)

        def send(k, _):
            px, pz = lax.rem(x + lax.rem(k, NX), NX), lax.rem(z + z_step(k // NX), NZ)
            pltpu.make_async_remote_copy(
                src_ref=sp.at[inner_index(px, pz, h)],
                dst_ref=rp.at[mine],
                send_sem=sp_sem.at[h],
                recv_sem=rp_sem,
                device_id={"latent": latent_index(px, pz, h)},
                device_id_type=MESH,
            ).start()
            return 0

        @pl.when(c == h)
        def _():
            pltpu.make_async_copy(sp.at[mine], rp.at[mine], rp_sem).start()

        @pl.when(c != h)
        def _():
            send(0, 0)

        lax.fori_loop(0, HALF - 1, lambda i, _: send(HALF - 1 - i, _), 0)

    with jax.named_scope("rows_first_part"):
        take(rx.at[pl.ds(0, 40)], rx_sem.at[0, 1])

    @pl.when(c == 1)
    def _():
        send_rows(sx, rx, sx_sem, rx_sem, None, OTHERS)

    with jax.named_scope("rows_of_core_0"):
        take(rx.at[pl.ds(0, 24)], rx_sem.at[0, 0])
    with jax.named_scope("forward_core_0"):
        forward(0)
    with jax.named_scope("rows_of_core_1"):
        take(rx.at[pl.ds(HALF, 40)], rx_sem.at[1, 1])
        take(rx.at[pl.ds(HALF, 24)], rx_sem.at[1, 0])
    with jax.named_scope("forward_core_1"):
        forward(1)

    with jax.named_scope("partials"):
        take(rp, rp_sem)

    for g in range(CAP * N // SUB):
        to_rows(rp, g % (N // SUB) * SUB, g // (N // SUB), nat, g * SUB)

    collect = smat[...].astype(F32).T.astype(BF16)

    def error(cols):
        recon = jnp.dot(collect, nat[:, cols], preferred_element_type=F32)
        err = (recon - tokens[:, cols].astype(F32)).astype(BF16)
        nat[:, cols] = jnp.dot(
            smat[...], err, preferred_element_type=F32
        ).astype(BF16)

    with jax.named_scope("error_rows"):
        for cols in pieces:
            error(cols)
        pack(se)
    with jax.named_scope("send_errors"):
        send_rows(se, re, se_sem, re_sem, 0, OTHERS)

    half_rows = NX * CHUNK

    def turned(values, h):
        return values[h].reshape(half_rows, LANE).astype(F32).T.astype(BF16)

    def arrived(h):
        with jax.named_scope("errors_of_core_%d" % h):
            take(re.at[pl.ds(h * HALF, 40)], re_sem.at[h, 1])
            take(re.at[pl.ds(h * HALF, 24)], re_sem.at[h, 0])
        unpack(re, enat, h)
        part_b[h] = contract(enat, dec, h)
        sent_b[h] = part_b[h].astype(BF16)
        for k in range(1, NY):
            pltpu.make_async_remote_copy(
                src_ref=sent_b.at[h],
                dst_ref=sum_b.at[h, k],
                send_sem=sf_sem.at[1, h],
                recv_sem=rf_sem.at[1, h],
                device_id={"tok": lax.rem(y + k, NY)},
                device_id_type=MESH,
            ).start()

    def finish(h):
        take(sum_b.at[h, pl.ds(1, NY - 1)], rf_sem.at[1, h])
        total = part_b[h]
        for k in range(1, NY):
            total = total + sum_b[h, k].astype(F32)
        back[h] = (mask_all[h].astype(F32) * total).astype(BF16)

    def half_product(left, other, h, cols):
        return jnp.dot(
            left, other[h * half_rows : (h + 1) * half_rows, cols], preferred_element_type=F32
        )

    code_rows = [turned(codes, h) for h in range(NC)]
    arrived(0)
    arrived(1)
    for h in range(NC):
        gathered(mask_all, h, 1)
    finish(0)
    for cols in pieces:
        gdec[:, cols] = (
            sum(half_product(code_rows[h], enat, h, cols) for h in range(NC))
        ).astype(BF16)
    left = turned(back, 0)
    for cols in pieces:
        early[:, cols] = half_product(left, xnat, 0, cols)
    finish(1)
    left = turned(back, 1)
    for cols in pieces:
        genc[:, cols] = (early[:, cols] + half_product(left, xnat, 1, cols)).astype(BF16)

    take(sx.at[pl.ds(0, N - 1)], sx_sem)
    take(se.at[pl.ds(0, N - 1)], se_sem)

    @pl.when(masked)
    def _():
        take(s1.at[pl.ds(0, NX - 1)], s1_sem)

        @pl.when(c == 0)
        def _():
            take(s1.at[0], s1_sem)

        @pl.when(c == 1)
        def _():
            take(s2.at[0], s2_sem)
            take(s2.at[1, pl.ds(0, NZ - 1)], s2_sem)

    for h in range(NC):

        @pl.when(c == h)
        def _(h=h):
            take(sp.at[pl.ds(0, HALF - 1)], sp_sem.at[h])

        @pl.when(c != h)
        def _(h=h):
            take(sp.at[pl.ds(0, HALF)], sp_sem.at[h])

        take(part_f.at[h, pl.ds(0, NY - 1)], sf_sem.at[0, h])
        take(sum_b.at[h, pl.ds(1, NY - 1)], sf_sem.at[1, h])
        take(codes.at[h, pl.ds(0, NY - 1)], sg_sem.at[0, h])
        take(mask_all.at[h, pl.ds(0, NY - 1)], sg_sem.at[1, h])


def local(tokens, blocks, slots, enc, dec, bias):
    rows, width = tokens.shape
    tiles = pltpu.VMEM((N, CAP, SUB, LANE), BF16)
    dense = pltpu.VMEM((CAP * N, width), BF16)
    shares = pltpu.VMEM((NC, NY, CHUNK, LANE), F32)
    shares16 = pltpu.VMEM((NC, NY, CHUNK, LANE), BF16)
    dma = pltpu.SemaphoreType.DMA
    hbm, vmem = pltpu.HBM, pltpu.VMEM
    args = (tokens, blocks.T, slots.T, enc, dec, bias.reshape(1, -1))
    genc, gdec = pl.pallas_call(
        kernel,
        out_shape=[jax.ShapeDtypeStruct((rows, width), BF16)] * 2,
        in_specs=[pl.BlockSpec(memory_space=hbm)] * 6,
        out_specs=[pl.BlockSpec(memory_space=vmem)] * 2,
        scratch_shapes=[pltpu.VMEM(a.shape, a.dtype) for a in args]
        + [tiles] * 6
        + [
            pltpu.VMEM((NX, NC * CHUNK, LANE), BF16),
            pltpu.VMEM((NC * NX, NC * CHUNK, LANE), BF16),
            pltpu.VMEM((NC, NZ, 2 * SUB, LANE), BF16),
            pltpu.VMEM((NY, 2 * SUB, LANE), BF16),
            dense,
            dense,
            dense,
            pltpu.VMEM((CAP * N, rows), BF16),
            pltpu.VMEM((rows, width), F32),
            shares,
            shares,
            shares,
            shares16,
            pltpu.VMEM((NC, NY, NY, CHUNK, LANE), BF16),
            shares16,
            shares16,
            pltpu.VMEM((NC, CHUNK, LANE), F32),
            shares16,
            dma,
            dma((NC,)),
            dma,
            dma,
            dma,
            dma((NC, 2)),
            dma,
            dma((NC, 2)),
            dma,
            dma,
            dma((2, NC)),
            dma((2, NC)),
            dma((2, NC)),
            dma((2, NC)),
            dma((6,)),
            pltpu.SemaphoreType.REGULAR,
        ],
        compiler_params=pltpu.CompilerParams(
            collective_id=0, has_side_effects=True, vmem_limit_bytes=36 << 20
        ),
    )(*[pltpu.with_memory_space_constraint(a, hbm) for a in args])
    scale = jnp.asarray(math.sqrt(LANE / (rows * slots.shape[1])), BF16)
    return genc * scale, gdec * scale


def solution(mesh):
    placed = (
        P("latent", "tok"),
        P("latent", None),
        P("latent", None),
        P("latent", "tok"),
        P("latent", "tok"),
        P("latent"),
    )
    return jax.shard_map(
        local,
        mesh=mesh,
        in_specs=placed,
        out_specs=(P("latent", "tok"), P("latent", "tok")),
        check_vma=False,
    )
```
